32 devices in a mesh: row: 8 (over z, y), col: 4 (over x, core).
Axes of the slice: x: 2, y: 2, z: 4, core: 2. Of those that a mesh axis runs over, the one named last changes fastest.
Arguments:
- queries: bfloat16 [1, 8, 8, 64, 2048], P(None, 'row', 'col'), may hold values from -17 to 17
- keys: bfloat16 [1, 8, 8, 64, 2048], P(None, 'row', 'col'), may hold values from -5.5 to 5.5
- values: bfloat16 [1, 8, 8, 64, 2048], P(None, 'row', 'col'), may hold values from -6 to 6
- pool_keys: bfloat16 [64, 16, 2048], P(('row', 'col')), may hold values from -6 to 6
- pool_values: bfloat16 [64, 16, 2048], P(('row', 'col')), may hold values from -6 to 6
- top_keys: bfloat16 [1, 32, 2048], P(None, 'col'), may hold values from -6 to 6
- top_values: bfloat16 [1, 32, 2048], P(None, 'col'), may hold values from -6 to 6
- coarse_ids: int32 [1, 8, 8, 8], P(None, 'row', 'col'), may hold values from 0 to 63, as said below
Outputs:
- attended: bfloat16 [1, 8, 8, 64, 2048], P(None, 'row', 'col')
The draws below stay inside these ranges and needn't reach their ends.
Inputs may be any that keep to these rules, and one draw needn't show every extreme that they name: Entry coarse_ids[n, i, j, c] names a pool block held by the device that holds fine block (i, j) or by one of its eight neighbours in the mesh (no wrap); the device with row index r and col index q holds pool blocks (r * 4 + q) * 2 to (r * 4 + q + 1) * 2 - 1. The 8 entries of a fine block differ.
All inputs are finite; a program needn't handle non-finite values.
Results may differ from the reference program's by a relative error of at most 0.0049.
Values may be sent and summed in bfloat16 or wider, within the bound.
A program may use at most 64 MiB of HBM per device.

```python
import math
import jax
import jax.numpy as jnp
from jax import lax

D = 2048
HEADS = 16
BT = 64
CT = 16
CB = 2
NCB = 8
IMAGES = 1
BR = 1
BC = 2
NBR = 8
NBC = 8
POOL = 64
TOP = 32


def query_key_pair(key):
    shape = (IMAGES, NBR, NBC, BT, D)
    query_seed = jax.random.fold_in(key, 11)
    key_seed = jax.random.fold_in(key, 12)
    keys_drawn = jnp.clip(jax.random.normal(key_seed, shape, jnp.float32), -4.0, 4.0)
    queries_drawn = 2.0 * jnp.clip(jax.random.normal(query_seed, shape, jnp.float32), -4.0, 4.0)
    return (queries_drawn, keys_drawn)


def draw_queries(key, part):
    return query_key_pair(key)[0].astype(jnp.bfloat16)


def draw_keys(key, part):
    return query_key_pair(key)[1].astype(jnp.bfloat16)


def draw_coarse_ids(key, part):
    slot_total = 9 * CB
    shape = (IMAGES, NBR, NBC, slot_total)
    mesh_rows = NBR // BR
    mesh_cols = NBC // BC
    slot_number = jnp.arange(slot_total, dtype=jnp.int32)
    offset_number = slot_number // CB
    row_shift = offset_number // 3 - 1
    col_shift = offset_number % 3 - 1
    local_number = slot_number % CB
    device_row = (jnp.arange(NBR, dtype=jnp.int32) // BR).reshape(1, NBR, 1, 1)
    device_col = (jnp.arange(NBC, dtype=jnp.int32) // BC).reshape(1, 1, NBC, 1)
    owner_row = device_row + row_shift
    owner_col = device_col + col_shift
    inside = (owner_row >= 0) & (owner_row < mesh_rows) & (owner_col >= 0) & (owner_col < mesh_cols)
    priority = jax.random.randint(jax.random.fold_in(key, 21), shape, 0, 2 ** 20, dtype=jnp.int32) * 64 + slot_number
    priority = jnp.where(inside, priority, priority - 2 ** 28)
    image_number = jnp.arange(IMAGES, dtype=jnp.int32).reshape(IMAGES, 1, 1, 1)
    block_row = jnp.arange(NBR, dtype=jnp.int32).reshape(1, NBR, 1, 1)
    block_col = jnp.arange(NBC, dtype=jnp.int32).reshape(1, 1, NBC, 1)
    first_pick = (image_number == 0) & (block_row == 0) & (block_col == 0) & (slot_number == 4 * CB)
    last_pick = (image_number == 0) & (block_row == NBR - 1) & (block_col == NBC - 1) & (slot_number == 5 * CB - 1)
    priority = priority + jnp.where(first_pick | last_pick, 2 ** 27, 0).astype(jnp.int32)
    chosen = lax.top_k(priority, NCB)[1]
    owner_device = owner_row * mesh_cols + owner_col
    full_ids = jnp.broadcast_to(owner_device * CB + local_number, shape).astype(jnp.int32)
    return jnp.take_along_axis(full_ids, chosen.astype(jnp.int32), axis=3).astype(jnp.int32)


def block_levels(key, extent, pieces, low, high):
    def one(axis_at, shards_of):
        steps = jax.random.uniform(jax.random.fold_in(jax.random.fold_in(key, 6), axis_at), (shards_of,), jnp.float32, low / len(pieces), high / len(pieces))
        return jnp.repeat(jnp.exp(steps), extent[axis_at] // shards_of).reshape((-1,) + (1,) * (len(extent) - axis_at - 1))

    gain = one(*pieces[0])
    for cut in pieces[1:]:
        gain = gain * one(*cut)
    return gain


def noise(stream_key, dims, deviation, bound, cuts=(), held_as=jnp.bfloat16):
    entries = deviation * jax.random.normal(stream_key, dims, jnp.float32)
    if cuts:
        entries = entries * block_levels(stream_key, dims, cuts, -0.22, 0.18)
    return jnp.clip(entries, -bound, bound).astype(held_as)


def setup_inputs(seed: int = 0) -> dict:
    key_list = jax.random.split(jax.random.key(seed), 9)
    queries = draw_queries(jax.random.fold_in(key_list[8], 71), 0)
    keys = draw_keys(jax.random.fold_in(key_list[8], 71), 0)
    values = noise(key_list[2], (IMAGES, NBR, NBC, BT, D), 1.0, 6.0, ((1, 8), (2, 4)))
    pool_keys = noise(key_list[3], (POOL, CT, D), 1.0, 6.0, ((0, 32),))
    pool_values = noise(key_list[4], (POOL, CT, D), 1.0, 6.0, ((0, 32),))
    top_keys = noise(key_list[5], (IMAGES, TOP, D), 1.0, 6.0, ((1, 4),))
    top_values = noise(key_list[6], (IMAGES, TOP, D), 1.0, 6.0, ((1, 4),))
    coarse_ids = draw_coarse_ids(jax.random.fold_in(key_list[8], 71), 0)
    return {"queries": queries, "keys": keys, "values": values, "pool_keys": pool_keys, "pool_values": pool_values, "top_keys": top_keys, "top_values": top_values, "coarse_ids": coarse_ids}


NEG_FILL = -1e+30

def reference(queries, keys, values, pool_keys, pool_values, top_keys, top_values, coarse_ids):
    head_width = D // HEADS
    score_scale = 1.0 / math.sqrt(head_width)
    padding = ((0, 0), (1, 1), (1, 1), (0, 0), (0, 0))
    padded_keys = jnp.pad(keys, padding)
    padded_values = jnp.pad(values, padding)
    column_number = jnp.arange(NBC, dtype=jnp.int32)

    def one_image(image_items):
        query_image, key_image, value_image, id_image, top_key_image, top_value_image = image_items
        top_key_heads = top_key_image.astype(jnp.float32).reshape(TOP, HEADS, head_width)
        top_value_heads = top_value_image.astype(jnp.float32).reshape(TOP, HEADS, head_width)

        def one_row(row_number):
            query_row = lax.dynamic_index_in_dim(query_image, row_number, 0, keepdims=False)
            query_row = query_row.astype(jnp.float32).reshape(NBC, BT, HEADS, head_width)
            key_rows = lax.dynamic_slice_in_dim(key_image, row_number, 3, 0)
            value_rows = lax.dynamic_slice_in_dim(value_image, row_number, 3, 0)
            id_row = lax.dynamic_index_in_dim(id_image, row_number, 0, keepdims=False)
            score_parts = []
            value_parts = []
            for row_step in range(3):
                row_valid = (row_number + row_step - 1 >= 0) & (row_number + row_step - 1 < NBR)
                for col_step in range(3):
                    col_valid = (column_number + col_step - 1 >= 0) & (column_number + col_step - 1 < NBC)
                    key_part = key_rows[row_step, col_step:col_step + NBC].astype(jnp.float32).reshape(NBC, BT, HEADS, head_width)
                    value_part = value_rows[row_step, col_step:col_step + NBC].astype(jnp.float32).reshape(NBC, BT, HEADS, head_width)
                    raw_scores = jnp.einsum('bqhd,bkhd->bhqk', query_row, key_part) * score_scale
                    valid_mask = (row_valid & col_valid).reshape(NBC, 1, 1, 1)
                    score_parts.append(jnp.where(valid_mask, raw_scores, NEG_FILL))
                    value_parts.append(value_part)
            coarse_keys = jnp.take(pool_keys, id_row, axis=0).astype(jnp.float32).reshape(NBC, NCB * CT, HEADS, head_width)
            coarse_values = jnp.take(pool_values, id_row, axis=0).astype(jnp.float32).reshape(NBC, NCB * CT, HEADS, head_width)
            score_parts.append(jnp.einsum('bqhd,bkhd->bhqk', query_row, coarse_keys) * score_scale)
            value_parts.append(coarse_values)
            score_parts.append(jnp.einsum('bqhd,khd->bhqk', query_row, top_key_heads) * score_scale)
            scores = jnp.concatenate(score_parts, axis=-1)
            row_peak = lax.optimization_barrier(jnp.max(scores, axis=-1, keepdims=True))
            exponent = jnp.exp(scores - row_peak)
            weights = lax.optimization_barrier((exponent / lax.optimization_barrier(jnp.sum(exponent, axis=-1, keepdims=True))).astype(jnp.bfloat16))
            weights = weights.astype(jnp.float32)
            result = jnp.zeros((NBC, BT, HEADS, head_width), jnp.float32)
            offset = 0
            for value_part in value_parts:
                length = value_part.shape[1]
                result = result + jnp.einsum('bhqk,bkhd->bqhd', weights[..., offset:offset + length], value_part)
                offset = offset + length
            result = result + jnp.einsum('bhqk,khd->bqhd', weights[..., offset:], top_value_heads)
            return result.reshape(NBC, BT, D).astype(jnp.bfloat16)
        return lax.map(one_row, jnp.arange(NBR, dtype=jnp.int32))
    return lax.map(one_image, (queries, padded_keys, padded_values, coarse_ids, top_keys, top_values))
```

```python
import functools
import math

import jax
import jax.numpy as jnp
from jax import lax
from jax.experimental import pallas as pl
from jax.experimental.pallas import tpu as pltpu
from jax.sharding import PartitionSpec as P

HEADS = 16
NEG_FILL = -1e30
HEADS_PER_CHUNK = 2
AHEAD = 2
OWN, NEAR, FAR = 0, 1, 2


def kernel(
    dims,
    q_in,
    k_in,
    v_in,
    pk_in,
    pv_in,
    tk_in,
    tv_in,
    ids,
    out,
    own,
    left,
    right,
    q_buf,
    out_buf,
    top,
    bias,
    load_sem,
    q_sem,
    out_sem,
    near_send,
    near_recv,
    far_send,
    far_recv,
    left_send,
    left_recv,
    right_send,
    right_recv,
    top_send,
    top_recv,
):
    rows, cols, tokens, pool_rows, pool_blocks, chunks, width, head_width = dims
    pool_tokens = pool_rows // pool_blocks
    r = lax.axis_index("row")
    c = lax.axis_index("col")
    odd = lax.rem(r, 2)
    near_row = r + 1 - 2 * odd
    far_row = r - 1 + 2 * odd
    far_to = r + 2 - 4 * odd
    has_far = (far_row >= 0) & (far_row < rows)
    has_to = (far_to >= 0) & (far_to < rows)
    has_left = c > 0
    has_right = c < cols - 1
    low = 2 * tokens
    mid = low + 2 * pool_rows
    full = mid + 2 * tokens
    edge = mid

    def lanes(g):
        return pl.ds(pl.multiple_of(g * width, width), width)

    def load_chunk(g, _):
        at = lanes(g)
        pieces = (
            (k_in.at[0, 0, 0, :, at], 0, tokens),
            (v_in.at[0, 0, 0, :, at], tokens, tokens),
            (k_in.at[0, 0, 1, :, at], mid, tokens),
            (v_in.at[0, 0, 1, :, at], mid + tokens, tokens),
        )
        for source, start, size in pieces:
            pltpu.make_async_copy(
                source, own.at[OWN, g, pl.ds(start, size)], load_sem.at[g]
            ).start()
        for block in range(pool_blocks):
            for source, start in ((pk_in, low), (pv_in, low + pool_rows)):
                pltpu.make_async_copy(
                    source.at[block, :, at],
                    own.at[OWN, g, pl.ds(start + block * pool_tokens, pool_tokens)],
                    load_sem.at[g],
                ).start()
        return 0

    barrier = pltpu.get_barrier_semaphore()

    def greet(there, row, col):
        @pl.when(there)
        def _():
            pl.semaphore_signal(
                barrier, inc=1, device_id=(row, col), device_id_type=pl.DeviceIdType.MESH
            )

    pl.semaphore_signal(
        barrier, inc=1, device_id=(near_row, c), device_id_type=pl.DeviceIdType.MESH
    )
    greet(r + 2 < rows, r + 2, c)
    greet(r >= 2, r - 2, c)
    for step in range(1, cols):
        pl.semaphore_signal(
            barrier,
            inc=1,
            device_id=(r, lax.rem(c + step, cols)),
            device_id_type=pl.DeviceIdType.MESH,
        )

    lax.fori_loop(0, chunks, load_chunk, 0)
    q_copy = pltpu.make_async_copy(q_in.at[0, 0], q_buf, q_sem)
    q_copy.start()

    top[c] = jnp.concatenate(
        [tk_in[0].astype(jnp.float32), tv_in[0].astype(jnp.float32)], axis=0
    ).astype(jnp.bfloat16)

    @pl.when(jnp.logical_not(has_far))
    def _():
        own[FAR] = jnp.zeros(own.shape[1:], own.dtype)

    @pl.when(jnp.logical_not(has_far & has_left))
    def _():
        left[FAR] = jnp.zeros(left.shape[1:], left.dtype)

    @pl.when(jnp.logical_not(has_far & has_right))
    def _():
        right[FAR] = jnp.zeros(right.shape[1:], right.dtype)

    @pl.when(jnp.logical_not(has_left))
    def _():
        for k in (OWN, NEAR):
            left[k] = jnp.zeros(left.shape[1:], left.dtype)

    @pl.when(jnp.logical_not(has_right))
    def _():
        for k in (OWN, NEAR):
            right[k] = jnp.zeros(right.shape[1:], right.dtype)

    top_rows = cols * tk_in.shape[1]
    for b in range(2):
        parts = []
        for k, row in ((OWN, r), (NEAR, near_row), (FAR, far_row)):
            row_there = (row >= 0) & (row < rows)
            for slot in range(4):
                if slot in (b, b + 1, b + 2):
                    there = row_there
                    if slot == 0:
                        there = there & has_left
                    if slot == 3:
                        there = there & has_right
                    value = jnp.where(there, 0.0, NEG_FILL)
                else:
                    value = jnp.float32(NEG_FILL)
                parts.append(jnp.full((1, tokens), value, jnp.float32))
            for shift in (-1, 0, 1):
                there = row_there & (c + shift >= 0) & (c + shift < cols)
                base = (row * cols + c + shift) * pool_blocks
                for block in range(pool_blocks):
                    listed_here = jnp.int32(0)
                    for n in range(ids.shape[3]):
                        listed_here = listed_here | (ids[0, 0, b, n] == base + block).astype(
                            jnp.int32
                        )
                    listed_here = listed_here * there.astype(jnp.int32)
                    value = (1.0 - listed_here.astype(jnp.float32)) * NEG_FILL
                    parts.append(jnp.full((1, pool_tokens), value, jnp.float32))
        parts.append(jnp.zeros((1, top_rows), jnp.float32))
        at = 0
        for part in parts:
            bias[b : b + 1, at : at + part.shape[1]] = part
            at += part.shape[1]

    greeted = (
        1
        + (r + 2 < rows).astype(jnp.int32)
        + (r >= 2).astype(jnp.int32)
        + (cols - 1)
    )
    pl.semaphore_wait(barrier, greeted)

    def remote(source, target, send, recv, row, col):
        return pltpu.make_async_remote_copy(
            src_ref=source,
            dst_ref=target,
            send_sem=send,
            recv_sem=recv,
            device_id=(row, col),
            device_id_type=pl.DeviceIdType.MESH,
        )

    def near_copy(g):
        return remote(
            own.at[OWN, g], own.at[NEAR, g], near_send, near_recv.at[g], near_row, c
        )

    def far_copy(g):
        return remote(own.at[NEAR, g], own.at[FAR, g], far_send, far_recv.at[g], far_to, c)

    def to_left(k, g):
        return remote(
            own.at[k, g, pl.ds(0, edge)],
            right.at[k, g],
            left_send.at[k],
            right_recv.at[k, g],
            r,
            c - 1,
        )

    def to_right(k, g):
        return remote(
            own.at[k, g, pl.ds(full - edge, edge)],
            left.at[k, g],
            right_send.at[k],
            left_recv.at[k, g],
            r,
            c + 1,
        )

    def sideways(k, g):
        @pl.when(has_left)
        def _():
            to_left(k, g).start()

        @pl.when(has_right)
        def _():
            to_right(k, g).start()

    def top_copy(step):
        to = lax.rem(c + step, cols)
        return remote(top.at[c], top.at[c], top_send.at[step], top_recv.at[step], r, to)

    def send_own(g):
        pltpu.make_async_copy(own.at[OWN, g], own.at[OWN, g], load_sem.at[g]).wait()
        near_copy(g).start()
        sideways(OWN, g)

    send_own(0)
    for step in range(1, cols):
        top_copy(step).start()
    for g in range(1, min(AHEAD, chunks)):
        send_own(g)
    q_copy.wait()

    score_scale = math.log2(math.e) / math.sqrt(head_width)

    def attend(g):
        at = lanes(g)
        q_chunk = q_buf[:, :, at].reshape(2 * tokens, width)
        tops = top[:, :, at].astype(jnp.float32)
        per = tk_in.shape[1]
        top_k = tops[:, :per].reshape(top_rows, width).astype(jnp.bfloat16)
        top_v = tops[:, per:].reshape(top_rows, width).astype(jnp.bfloat16)

        def listed(head, value, top_part):
            lane = pl.ds(head * head_width, head_width)
            fine = tokens if value else 0
            pool = pool_rows if value else 0
            side = full - edge
            parts = []
            for k in (OWN, NEAR, FAR):
                parts += [
                    left[k, g, pl.ds(mid + fine - side, tokens), lane],
                    own[k, g, pl.ds(fine, tokens), lane],
                    own[k, g, pl.ds(mid + fine, tokens), lane],
                    right[k, g, pl.ds(fine, tokens), lane],
                    left[k, g, pl.ds(low + pool - side, pool_rows), lane],
                    own[k, g, pl.ds(low + pool, pool_rows), lane],
                    right[k, g, pl.ds(low + pool, pool_rows), lane],
                ]
            parts.append(top_part[:, head * head_width : (head + 1) * head_width])
            return jnp.concatenate(parts, axis=0)

        for head in range(width // head_width):
            q_head = q_chunk[:, head * head_width : (head + 1) * head_width]
            scores = lax.dot_general(
                q_head,
                listed(head, False, top_k),
                (((1,), (1,)), ((), ())),
                preferred_element_type=jnp.float32,
            )
            scores = (scores * score_scale).reshape(2, tokens, -1) + bias[...][:, None, :]
            peak = jnp.max(scores, axis=-1, keepdims=True)
            exponent = jnp.exp2(scores - peak)
            total = jnp.sum(exponent, axis=-1, keepdims=True)
            weights = (exponent * (1.0 / total)).astype(jnp.bfloat16)
            result = jnp.dot(
                weights.reshape(2 * tokens, -1),
                listed(head, True, top_v),
                preferred_element_type=jnp.float32,
            )
            out_buf[g, :, :, head * head_width : (head + 1) * head_width] = result.reshape(
                2, tokens, head_width
            ).astype(jnp.bfloat16)
        pltpu.make_async_copy(out_buf.at[g], out.at[0, 0, :, :, at], out_sem).start()

    def step(t, _):
        @pl.when(t < chunks)
        def _():
            near_copy(t).wait_recv()

            @pl.when(has_to)
            def _():
                far_copy(t).start()

            sideways(NEAR, t)

        @pl.when(t + AHEAD < chunks)
        def _():
            send_own(t + AHEAD)

        @pl.when((t >= 1) & (t <= chunks) & has_far)
        def _():
            far_copy(t - 1).wait_recv()
            sideways(FAR, t - 1)

        @pl.when(t >= 2)
        def _():
            g = t - 2

            @pl.when(g == 0)
            def _():
                for s in range(1, cols):
                    top_copy(s).wait_recv()

            @pl.when(has_left)
            def _():
                to_right(OWN, g).wait_recv()
                to_right(NEAR, g).wait_recv()

            @pl.when(has_right)
            def _():
                to_left(OWN, g).wait_recv()
                to_left(NEAR, g).wait_recv()

            @pl.when(has_far & has_left)
            def _():
                to_right(FAR, g).wait_recv()

            @pl.when(has_far & has_right)
            def _():
                to_left(FAR, g).wait_recv()

            attend(g)

        return 0

    lax.fori_loop(0, chunks + 2, step, 0)

    remote(own.at[OWN], own.at[NEAR], near_send, near_recv.at[0], near_row, c).wait_send()

    @pl.when(has_to)
    def _():
        remote(own.at[NEAR], own.at[FAR], far_send, far_recv.at[0], far_to, c).wait_send()

    def sent(k):
        @pl.when(has_left)
        def _():
            remote(
                own.at[k, :, pl.ds(0, edge)],
                right.at[k],
                left_send.at[k],
                right_recv.at[k, 0],
                r,
                c - 1,
            ).wait_send()

        @pl.when(has_right)
        def _():
            remote(
                own.at[k, :, pl.ds(full - edge, edge)],
                left.at[k],
                right_send.at[k],
                left_recv.at[k, 0],
                r,
                c + 1,
            ).wait_send()

    sent(OWN)
    sent(NEAR)

    @pl.when(has_far)
    def _():
        sent(FAR)

    for s in range(1, cols):
        top_copy(s).wait_send()
    pltpu.make_async_copy(out_buf, out_buf, out_sem).wait()


def solution(mesh):
    row_count, col_count = mesh.shape["row"], mesh.shape["col"]

    def body(queries, keys, values, pool_keys, pool_values, top_keys, top_values, coarse_ids):
        tokens, model_width = queries.shape[3:]
        pool_blocks, pool_tokens, _ = pool_keys.shape
        pool_rows = pool_blocks * pool_tokens
        head_width = model_width // HEADS
        width = HEADS_PER_CHUNK * head_width
        chunks = model_width // width
        full = 4 * tokens + 2 * pool_rows
        edge = 2 * tokens + 2 * pool_rows
        per = top_keys.shape[1]
        listed = 3 * (4 * tokens + 3 * pool_rows) + col_count * per
        dims = (row_count, col_count, tokens, pool_rows, pool_blocks, chunks, width, head_width)
        dma = pltpu.SemaphoreType.DMA
        return pl.pallas_call(
            functools.partial(kernel, dims),
            out_shape=jax.ShapeDtypeStruct(queries.shape, queries.dtype),
            in_specs=[pl.BlockSpec(memory_space=pl.ANY)] * 5
            + [pl.BlockSpec(memory_space=pltpu.VMEM)] * 2
            + [pl.BlockSpec(memory_space=pltpu.SMEM)],
            out_specs=pl.BlockSpec(memory_space=pl.ANY),
            scratch_shapes=[
                pltpu.VMEM((3, chunks, full, width), jnp.bfloat16),
                pltpu.VMEM((3, chunks, edge, width), jnp.bfloat16),
                pltpu.VMEM((3, chunks, edge, width), jnp.bfloat16),
                pltpu.VMEM((2, tokens, model_width), jnp.bfloat16),
                pltpu.VMEM((chunks, 2, tokens, width), jnp.bfloat16),
                pltpu.VMEM((col_count, 2 * per, model_width), jnp.bfloat16),
                pltpu.VMEM((2, listed), jnp.float32),
                dma((chunks,)),
                dma,
                dma,
                dma,
                dma((chunks,)),
                dma,
                dma((chunks,)),
                dma((3,)),
                dma((3, chunks)),
                dma((3,)),
                dma((3, chunks)),
                dma((col_count,)),
                dma((col_count,)),
            ],
            compiler_params=pltpu.CompilerParams(
                collective_id=0, has_side_effects=True, vmem_limit_bytes=40 * 2**20
            ),
            cost_estimate=pl.CostEstimate(
                flops=4 * 2 * tokens * listed * model_width,
                bytes_accessed=8 * 2**20,
                transcendentals=2 * tokens * listed * HEADS,
            ),
        )(queries, keys, values, pool_keys, pool_values, top_keys, top_values, coarse_ids)

    placed = (
        P(None, "row", "col", None, None),
        P(None, "row", "col", None, None),
        P(None, "row", "col", None, None),
        P(("row", "col"), None, None),
        P(("row", "col"), None, None),
        P(None, "col", None),
        P(None, "col", None),
        P(None, "row", "col", None),
    )
    return jax.shard_map(
        body,
        mesh=mesh,
        in_specs=placed,
        out_specs=P(None, "row", "col", None, None),
        check_vma=False,
    )
```

```python
import functools
import math

import jax
import jax.numpy as jnp
from jax import lax
from jax.experimental import pallas as pl
from jax.experimental.pallas import tpu as pltpu
from jax.sharding import PartitionSpec as P

HEADS = 16
NEG_FILL = -1e30
HEADS_PER_CHUNK = 2
AHEAD = 2
OWN, NEAR, FAR = 0, 1, 2


def kernel(
    dims,
    q_in,
    k_in,
    v_in,
    pk_in,
    pv_in,
    tk_in,
    tv_in,
    ids_in,
    out,
    own,
    left,
    right,
    q_buf,
    out_buf,
    top,
    top_own,
    ids,
    bias,
    load_sem,
    top_sem,
    ids_sem,
    q_sem,
    out_sem,
    near_send,
    near_recv,
    far_send,
    far_recv,
    left_send,
    left_recv,
    right_send,
    right_recv,
    top_send,
    top_recv,
):
    rows, cols, tokens, pool_rows, pool_blocks, chunks, width, head_width = dims
    pool_tokens = pool_rows // pool_blocks
    r = lax.axis_index("row")
    c = lax.axis_index("col")
    odd = lax.rem(r, 2)
    near_row = r + 1 - 2 * odd
    far_row = r - 1 + 2 * odd
    far_to = r + 2 - 4 * odd
    has_far = (far_row >= 0) & (far_row < rows)
    has_to = (far_to >= 0) & (far_to < rows)
    has_left = c > 0
    has_right = c < cols - 1
    low = 2 * tokens
    mid = low + 2 * pool_rows
    full = mid + 2 * tokens
    edge = mid

    def lanes(g):
        return pl.ds(pl.multiple_of(g * width, width), width)

    def load_chunk(g, _):
        at = lanes(g)
        pieces = (
            (k_in.at[0, 0, 0, :, at], 0, tokens),
            (v_in.at[0, 0, 0, :, at], tokens, tokens),
            (k_in.at[0, 0, 1, :, at], mid, tokens),
            (v_in.at[0, 0, 1, :, at], mid + tokens, tokens),
        )
        for source, start, size in pieces:
            pltpu.make_async_copy(
                source, own.at[OWN, g, pl.ds(start, size)], load_sem.at[g]
            ).start()
        for block in range(pool_blocks):
            for source, start in ((pk_in, low), (pv_in, low + pool_rows)):
                pltpu.make_async_copy(
                    source.at[block, :, at],
                    own.at[OWN, g, pl.ds(start + block * pool_tokens, pool_tokens)],
                    load_sem.at[g],
                ).start()
        return 0

    barrier = pltpu.get_barrier_semaphore()

    def greet(there, row, col):
        @pl.when(there)
        def _():
            pl.semaphore_signal(
                barrier, inc=1, device_id=(row, col), device_id_type=pl.DeviceIdType.MESH
            )

    pl.semaphore_signal(
        barrier, inc=1, device_id=(near_row, c), device_id_type=pl.DeviceIdType.MESH
    )
    greet(r + 2 < rows, r + 2, c)
    greet(r >= 2, r - 2, c)
    for step in range(1, cols):
        pl.semaphore_signal(
            barrier,
            inc=1,
            device_id=(r, lax.rem(c + step, cols)),
            device_id_type=pl.DeviceIdType.MESH,
        )

    ids_copy = pltpu.make_async_copy(ids_in, ids, ids_sem)
    ids_copy.start()
    tk_copy = pltpu.make_async_copy(tk_in.at[0], top_own.at[0], top_sem.at[0])
    tk_copy.start()
    tv_copy = pltpu.make_async_copy(tv_in.at[0], top_own.at[1], top_sem.at[1])
    tv_copy.start()
    lax.fori_loop(0, chunks, load_chunk, 0)
    q_copy = pltpu.make_async_copy(q_in.at[0, 0], q_buf, q_sem)
    q_copy.start()

    tk_copy.wait()
    tv_copy.wait()
    ids_copy.wait()
    top[c] = jnp.concatenate(
        [top_own[0].astype(jnp.float32), top_own[1].astype(jnp.float32)], axis=0
    ).astype(jnp.bfloat16)

    @pl.when(jnp.logical_not(has_far))
    def _():
        own[FAR] = jnp.zeros(own.shape[1:], own.dtype)

    @pl.when(jnp.logical_not(has_far & has_left))
    def _():
        left[FAR] = jnp.zeros(left.shape[1:], left.dtype)

    @pl.when(jnp.logical_not(has_far & has_right))
    def _():
        right[FAR] = jnp.zeros(right.shape[1:], right.dtype)

    @pl.when(jnp.logical_not(has_left))
    def _():
        for k in (OWN, NEAR):
            left[k] = jnp.zeros(left.shape[1:], left.dtype)

    @pl.when(jnp.logical_not(has_right))
    def _():
        for k in (OWN, NEAR):
            right[k] = jnp.zeros(right.shape[1:], right.dtype)

    top_rows = cols * tk_in.shape[1]
    for b in range(2):
        parts = []
        for k, row in ((OWN, r), (NEAR, near_row), (FAR, far_row)):
            row_there = (row >= 0) & (row < rows)
            for slot in range(4):
                if slot in (b, b + 1, b + 2):
                    there = row_there
                    if slot == 0:
                        there = there & has_left
                    if slot == 3:
                        there = there & has_right
                    value = jnp.where(there, 0.0, NEG_FILL)
                else:
                    value = jnp.float32(NEG_FILL)
                parts.append(jnp.full((1, tokens), value, jnp.float32))
            for shift in (-1, 0, 1):
                there = row_there & (c + shift >= 0) & (c + shift < cols)
                base = (row * cols + c + shift) * pool_blocks
                for block in range(pool_blocks):
                    listed_here = jnp.int32(0)
                    for n in range(ids.shape[3]):
                        listed_here = listed_here | (ids[0, 0, b, n] == base + block).astype(
                            jnp.int32
                        )
                    listed_here = listed_here * there.astype(jnp.int32)
                    value = (1.0 - listed_here.astype(jnp.float32)) * NEG_FILL
                    parts.append(jnp.full((1, pool_tokens), value, jnp.float32))
        parts.append(jnp.zeros((1, top_rows), jnp.float32))
        at = 0
        for part in parts:
            bias[b : b + 1, at : at + part.shape[1]] = part
            at += part.shape[1]

    greeted = (
        1
        + (r + 2 < rows).astype(jnp.int32)
        + (r >= 2).astype(jnp.int32)
        + (cols - 1)
    )
    pl.semaphore_wait(barrier, greeted)

    def remote(source, target, send, recv, row, col):
        return pltpu.make_async_remote_copy(
            src_ref=source,
            dst_ref=target,
            send_sem=send,
            recv_sem=recv,
            device_id=(row, col),
            device_id_type=pl.DeviceIdType.MESH,
        )

    def near_copy(g):
        return remote(
            own.at[OWN, g], own.at[NEAR, g], near_send, near_recv.at[g], near_row, c
        )

    def far_copy(g):
        return remote(own.at[NEAR, g], own.at[FAR, g], far_send, far_recv.at[g], far_to, c)

    def to_left(k, g):
        return remote(
            own.at[k, g, pl.ds(0, edge)],
            right.at[k, g],
            left_send.at[k],
            right_recv.at[k, g],
            r,
            c - 1,
        )

    def to_right(k, g):
        return remote(
            own.at[k, g, pl.ds(full - edge, edge)],
            left.at[k, g],
            right_send.at[k],
            left_recv.at[k, g],
            r,
            c + 1,
        )

    def sideways(k, g):
        @pl.when(has_left)
        def _():
            to_left(k, g).start()

        @pl.when(has_right)
        def _():
            to_right(k, g).start()

    def top_copy(step):
        to = lax.rem(c + step, cols)
        return remote(top.at[c], top.at[c], top_send.at[step], top_recv.at[step], r, to)

    def send_own(g):
        pltpu.make_async_copy(own.at[OWN, g], own.at[OWN, g], load_sem.at[g]).wait()
        near_copy(g).start()
        sideways(OWN, g)

    send_own(0)
    for step in range(1, cols):
        top_copy(step).start()
    for g in range(1, min(AHEAD, chunks)):
        send_own(g)
    q_copy.wait()

    score_scale = math.log2(math.e) / math.sqrt(head_width)

    def attend(g):
        at = lanes(g)
        q_chunk = q_buf[:, :, at].reshape(2 * tokens, width)
        tops = top[:, :, at].astype(jnp.float32)
        per = tk_in.shape[1]
        top_k = tops[:, :per].reshape(top_rows, width).astype(jnp.bfloat16)
        top_v = tops[:, per:].reshape(top_rows, width).astype(jnp.bfloat16)

        def listed(head, value, top_part):
            lane = pl.ds(head * head_width, head_width)
            fine = tokens if value else 0
            pool = pool_rows if value else 0
            side = full - edge
            parts = []
            for k in (OWN, NEAR, FAR):
                parts += [
                    left[k, g, pl.ds(mid + fine - side, tokens), lane],
                    own[k, g, pl.ds(fine, tokens), lane],
                    own[k, g, pl.ds(mid + fine, tokens), lane],
                    right[k, g, pl.ds(fine, tokens), lane],
                    left[k, g, pl.ds(low + pool - side, pool_rows), lane],
                    own[k, g, pl.ds(low + pool, pool_rows), lane],
                    right[k, g, pl.ds(low + pool, pool_rows), lane],
                ]
            parts.append(top_part[:, head * head_width : (head + 1) * head_width])
            return jnp.concatenate(parts, axis=0)

        for head in range(width // head_width):
            q_head = q_chunk[:, head * head_width : (head + 1) * head_width]
            scores = lax.dot_general(
                q_head,
                listed(head, False, top_k),
                (((1,), (1,)), ((), ())),
                preferred_element_type=jnp.float32,
            )
            scores = (scores * score_scale).reshape(2, tokens, -1) + bias[...][:, None, :]
            peak = jnp.max(scores, axis=-1, keepdims=True)
            exponent = jnp.exp2(scores - peak)
            total = jnp.sum(exponent, axis=-1, keepdims=True)
            weights = (exponent * (1.0 / total)).astype(jnp.bfloat16)
            result = jnp.dot(
                weights.reshape(2 * tokens, -1),
                listed(head, True, top_v),
                preferred_element_type=jnp.float32,
            )
            out_buf[g, :, :, head * head_width : (head + 1) * head_width] = result.reshape(
                2, tokens, head_width
            ).astype(jnp.bfloat16)
        pltpu.make_async_copy(out_buf.at[g], out.at[0, 0, :, :, at], out_sem).start()

    def step(t, _):
        @pl.when(t < chunks)
        def _():
            near_copy(t).wait_recv()

            @pl.when(has_to)
            def _():
                far_copy(t).start()

            sideways(NEAR, t)

        @pl.when(t + AHEAD < chunks)
        def _():
            send_own(t + AHEAD)

        @pl.when((t >= 1) & (t <= chunks) & has_far)
        def _():
            far_copy(t - 1).wait_recv()
            sideways(FAR, t - 1)

        @pl.when(t >= 2)
        def _():
            g = t - 2

            @pl.when(g == 0)
            def _():
                for s in range(1, cols):
                    top_copy(s).wait_recv()

            @pl.when(has_left)
            def _():
                to_right(OWN, g).wait_recv()
                to_right(NEAR, g).wait_recv()

            @pl.when(has_right)
            def _():
                to_left(OWN, g).wait_recv()
                to_left(NEAR, g).wait_recv()

            @pl.when(has_far & has_left)
            def _():
                to_right(FAR, g).wait_recv()

            @pl.when(has_far & has_right)
            def _():
                to_left(FAR, g).wait_recv()

            attend(g)

        return 0

    lax.fori_loop(0, chunks + 2, step, 0)

    remote(own.at[OWN], own.at[NEAR], near_send, near_recv.at[0], near_row, c).wait_send()

    @pl.when(has_to)
    def _():
        remote(own.at[NEAR], own.at[FAR], far_send, far_recv.at[0], far_to, c).wait_send()

    def sent(k):
        @pl.when(has_left)
        def _():
            remote(
                own.at[k, :, pl.ds(0, edge)],
                right.at[k],
                left_send.at[k],
                right_recv.at[k, 0],
                r,
                c - 1,
            ).wait_send()

        @pl.when(has_right)
        def _():
            remote(
                own.at[k, :, pl.ds(full - edge, edge)],
                left.at[k],
                right_send.at[k],
                left_recv.at[k, 0],
                r,
                c + 1,
            ).wait_send()

    sent(OWN)
    sent(NEAR)

    @pl.when(has_far)
    def _():
        sent(FAR)

    for s in range(1, cols):
        top_copy(s).wait_send()
    pltpu.make_async_copy(out_buf, out_buf, out_sem).wait()


def solution(mesh):
    row_count, col_count = mesh.shape["row"], mesh.shape["col"]

    def body(queries, keys, values, pool_keys, pool_values, top_keys, top_values, coarse_ids):
        tokens, model_width = queries.shape[3:]
        pool_blocks, pool_tokens, _ = pool_keys.shape
        pool_rows = pool_blocks * pool_tokens
        head_width = model_width // HEADS
        width = HEADS_PER_CHUNK * head_width
        chunks = model_width // width
        full = 4 * tokens + 2 * pool_rows
        edge = 2 * tokens + 2 * pool_rows
        per = top_keys.shape[1]
        listed = 3 * (4 * tokens + 3 * pool_rows) + col_count * per
        dims = (row_count, col_count, tokens, pool_rows, pool_blocks, chunks, width, head_width)
        dma = pltpu.SemaphoreType.DMA
        return pl.pallas_call(
            functools.partial(kernel, dims),
            out_shape=jax.ShapeDtypeStruct(queries.shape, queries.dtype),
            in_specs=[pl.BlockSpec(memory_space=pltpu.HBM)] * 8,
            out_specs=pl.BlockSpec(memory_space=pl.ANY),
            scratch_shapes=[
                pltpu.VMEM((3, chunks, full, width), jnp.bfloat16),
                pltpu.VMEM((3, chunks, edge, width), jnp.bfloat16),
                pltpu.VMEM((3, chunks, edge, width), jnp.bfloat16),
                pltpu.VMEM((2, tokens, model_width), jnp.bfloat16),
                pltpu.VMEM((chunks, 2, tokens, width), jnp.bfloat16),
                pltpu.VMEM((col_count, 2 * per, model_width), jnp.bfloat16),
                pltpu.VMEM((2, per, model_width), jnp.bfloat16),
                pltpu.SMEM(coarse_ids.shape, jnp.int32),
                pltpu.VMEM((2, listed), jnp.float32),
                dma((chunks,)),
                dma((2,)),
                dma,
                dma,
                dma,
                dma,
                dma((chunks,)),
                dma,
                dma((chunks,)),
                dma((3,)),
                dma((3, chunks)),
                dma((3,)),
                dma((3, chunks)),
                dma((col_count,)),
                dma((col_count,)),
            ],
            compiler_params=pltpu.CompilerParams(
                collective_id=0, has_side_effects=True, vmem_limit_bytes=63 * 2**20
            ),
            cost_estimate=pl.CostEstimate(
                flops=4 * 2 * tokens * listed * model_width,
                bytes_accessed=8 * 2**20,
                transcendentals=2 * tokens * listed * HEADS,
            ),
        )(queries, keys, values, pool_keys, pool_values, top_keys, top_values, coarse_ids)

    placed = (
        P(None, "row", "col", None, None),
        P(None, "row", "col", None, None),
        P(None, "row", "col", None, None),
        P(("row", "col"), None, None),
        P(("row", "col"), None, None),
        P(None, "col", None),
        P(None, "col", None),
        P(None, "row", "col", None),
    )
    return jax.shard_map(
        body,
        mesh=mesh,
        in_specs=placed,
        out_specs=P(None, "row", "col", None, None),
        check_vma=False,
    )
```

```python
import functools
import math

import jax
import jax.numpy as jnp
from jax import lax
from jax.experimental import pallas as pl
from jax.experimental.pallas import tpu as pltpu
from jax.sharding import PartitionSpec as P

HEADS = 16
NEG_FILL = -1e30
HEADS_PER_CHUNK = 1
AHEAD = 2
OWN, NEAR, FAR = 0, 1, 2


def kernel(
    dims,
    q_in,
    k_in,
    v_in,
    pk_in,
    pv_in,
    tk_in,
    tv_in,
    ids_in,
    out,
    own,
    left,
    right,
    q_buf,
    out_buf,
    top,
    top_own,
    ids,
    bias,
    load_sem,
    top_sem,
    ids_sem,
    q_sem,
    out_sem,
    near_send,
    near_recv,
    far_send,
    far_recv,
    left_send,
    left_recv,
    right_send,
    right_recv,
    top_send,
    top_recv,
):
    rows, cols, tokens, pool_rows, pool_blocks, chunks, width, head_width = dims
    pool_tokens = pool_rows // pool_blocks
    r = lax.axis_index("row")
    c = lax.axis_index("col")
    odd = lax.rem(r, 2)
    near_row = r + 1 - 2 * odd
    far_row = r - 1 + 2 * odd
    far_to = r + 2 - 4 * odd
    has_far = (far_row >= 0) & (far_row < rows)
    has_to = (far_to >= 0) & (far_to < rows)
    has_left = c > 0
    has_right = c < cols - 1
    low = 2 * tokens
    mid = low + 2 * pool_rows
    full = mid + 2 * tokens
    edge = mid

    def lanes(g):
        return pl.ds(pl.multiple_of(g * width, width), width)

    def load_chunk(g, _):
        at = lanes(g)
        pieces = (
            (k_in.at[0, 0, 0, :, at], 0, tokens),
            (v_in.at[0, 0, 0, :, at], tokens, tokens),
            (k_in.at[0, 0, 1, :, at], mid, tokens),
            (v_in.at[0, 0, 1, :, at], mid + tokens, tokens),
        )
        for source, start, size in pieces:
            pltpu.make_async_copy(
                source, own.at[OWN, g, pl.ds(start, size)], load_sem.at[g]
            ).start()
        for block in range(pool_blocks):
            for source, start in ((pk_in, low), (pv_in, low + pool_rows)):
                pltpu.make_async_copy(
                    source.at[block, :, at],
                    own.at[OWN, g, pl.ds(start + block * pool_tokens, pool_tokens)],
                    load_sem.at[g],
                ).start()
        return 0

    barrier = pltpu.get_barrier_semaphore()

    def greet(there, row, col):
        @pl.when(there)
        def _():
            pl.semaphore_signal(
                barrier, inc=1, device_id=(row, col), device_id_type=pl.DeviceIdType.MESH
            )

    pl.semaphore_signal(
        barrier, inc=1, device_id=(near_row, c), device_id_type=pl.DeviceIdType.MESH
    )
    greet(r + 2 < rows, r + 2, c)
    greet(r >= 2, r - 2, c)
    for step in range(1, cols):
        pl.semaphore_signal(
            barrier,
            inc=1,
            device_id=(r, lax.rem(c + step, cols)),
            device_id_type=pl.DeviceIdType.MESH,
        )

    ids_copy = pltpu.make_async_copy(ids_in, ids, ids_sem)
    ids_copy.start()
    tk_copy = pltpu.make_async_copy(tk_in.at[0], top_own.at[0], top_sem.at[0])
    tk_copy.start()
    tv_copy = pltpu.make_async_copy(tv_in.at[0], top_own.at[1], top_sem.at[1])
    tv_copy.start()
    lax.fori_loop(0, chunks, load_chunk, 0)
    q_copy = pltpu.make_async_copy(q_in.at[0, 0], q_buf, q_sem)
    q_copy.start()

    tk_copy.wait()
    tv_copy.wait()
    ids_copy.wait()
    top[c] = jnp.concatenate(
        [top_own[0].astype(jnp.float32), top_own[1].astype(jnp.float32)], axis=0
    ).astype(jnp.bfloat16)

    @pl.when(jnp.logical_not(has_far))
    def _():
        own[FAR] = jnp.zeros(own.shape[1:], own.dtype)

    @pl.when(jnp.logical_not(has_far & has_left))
    def _():
        left[FAR] = jnp.zeros(left.shape[1:], left.dtype)

    @pl.when(jnp.logical_not(has_far & has_right))
    def _():
        right[FAR] = jnp.zeros(right.shape[1:], right.dtype)

    @pl.when(jnp.logical_not(has_left))
    def _():
        for k in (OWN, NEAR):
            left[k] = jnp.zeros(left.shape[1:], left.dtype)

    @pl.when(jnp.logical_not(has_right))
    def _():
        for k in (OWN, NEAR):
            right[k] = jnp.zeros(right.shape[1:], right.dtype)

    top_rows = cols * tk_in.shape[1]
    for b in range(2):
        parts = []
        for k, row in ((OWN, r), (NEAR, near_row), (FAR, far_row)):
            row_there = (row >= 0) & (row < rows)
            for slot in range(4):
                if slot in (b, b + 1, b + 2):
                    there = row_there
                    if slot == 0:
                        there = there & has_left
                    if slot == 3:
                        there = there & has_right
                    value = jnp.where(there, 0.0, NEG_FILL)
                else:
                    value = jnp.float32(NEG_FILL)
                parts.append(jnp.full((1, tokens), value, jnp.float32))
            for shift in (-1, 0, 1):
                there = row_there & (c + shift >= 0) & (c + shift < cols)
                base = (row * cols + c + shift) * pool_blocks
                for block in range(pool_blocks):
                    listed_here = jnp.int32(0)
                    for n in range(ids.shape[3]):
                        listed_here = listed_here | (ids[0, 0, b, n] == base + block).astype(
                            jnp.int32
                        )
                    listed_here = listed_here * there.astype(jnp.int32)
                    value = (1.0 - listed_here.astype(jnp.float32)) * NEG_FILL
                    parts.append(jnp.full((1, pool_tokens), value, jnp.float32))
        parts.append(jnp.zeros((1, top_rows), jnp.float32))
        at = 0
        for part in parts:
            bias[b : b + 1, at : at + part.shape[1]] = part
            at += part.shape[1]

    greeted = (
        1
        + (r + 2 < rows).astype(jnp.int32)
        + (r >= 2).astype(jnp.int32)
        + (cols - 1)
    )
    pl.semaphore_wait(barrier, greeted)

    def remote(source, target, send, recv, row, col):
        return pltpu.make_async_remote_copy(
            src_ref=source,
            dst_ref=target,
            send_sem=send,
            recv_sem=recv,
            device_id=(row, col),
            device_id_type=pl.DeviceIdType.MESH,
        )

    def near_copy(g):
        return remote(
            own.at[OWN, g], own.at[NEAR, g], near_send, near_recv.at[g], near_row, c
        )

    def far_copy(g):
        return remote(own.at[NEAR, g], own.at[FAR, g], far_send, far_recv.at[g], far_to, c)

    def to_left(k, g):
        return remote(
            own.at[k, g, pl.ds(0, edge)],
            right.at[k, g],
            left_send.at[k],
            right_recv.at[k, g],
            r,
            c - 1,
        )

    def to_right(k, g):
        return remote(
            own.at[k, g, pl.ds(full - edge, edge)],
            left.at[k, g],
            right_send.at[k],
            left_recv.at[k, g],
            r,
            c + 1,
        )

    def sideways(k, g):
        @pl.when(has_left)
        def _():
            to_left(k, g).start()

        @pl.when(has_right)
        def _():
            to_right(k, g).start()

    def top_copy(step):
        to = lax.rem(c + step, cols)
        return remote(top.at[c], top.at[c], top_send.at[step], top_recv.at[step], r, to)

    def send_own(g):
        pltpu.make_async_copy(own.at[OWN, g], own.at[OWN, g], load_sem.at[g]).wait()
        near_copy(g).start()
        sideways(OWN, g)

    send_own(0)
    for step in range(1, cols):
        top_copy(step).start()
    for g in range(1, min(AHEAD, chunks)):
        send_own(g)
    q_copy.wait()

    score_scale = math.log2(math.e) / math.sqrt(head_width)

    def attend(g):
        at = lanes(g)
        q_chunk = q_buf[:, :, at].reshape(2 * tokens, width)
        tops = top[:, :, at].astype(jnp.float32)
        per = tk_in.shape[1]
        top_k = tops[:, :per].reshape(top_rows, width).astype(jnp.bfloat16)
        top_v = tops[:, per:].reshape(top_rows, width).astype(jnp.bfloat16)

        def listed(head, value, top_part):
            lane = pl.ds(head * head_width, head_width)
            fine = tokens if value else 0
            pool = pool_rows if value else 0
            side = full - edge
            parts = []
            for k in (OWN, NEAR, FAR):
                parts += [
                    left[k, g, pl.ds(mid + fine - side, tokens), lane],
                    own[k, g, pl.ds(fine, tokens), lane],
                    own[k, g, pl.ds(mid + fine, tokens), lane],
                    right[k, g, pl.ds(fine, tokens), lane],
                    left[k, g, pl.ds(low + pool - side, pool_rows), lane],
                    own[k, g, pl.ds(low + pool, pool_rows), lane],
                    right[k, g, pl.ds(low + pool, pool_rows), lane],
                ]
            parts.append(top_part[:, head * head_width : (head + 1) * head_width])
            return jnp.concatenate(parts, axis=0)

        for head in range(width // head_width):
            q_head = q_chunk[:, head * head_width : (head + 1) * head_width]
            scores = lax.dot_general(
                q_head,
                listed(head, False, top_k),
                (((1,), (1,)), ((), ())),
                preferred_element_type=jnp.float32,
            )
            scores = (scores * score_scale).reshape(2, tokens, -1) + bias[...][:, None, :]
            peak = jnp.max(scores, axis=-1, keepdims=True)
            exponent = jnp.exp2(scores - peak)
            total = jnp.sum(exponent, axis=-1, keepdims=True)
            weights = (exponent * (1.0 / total)).astype(jnp.bfloat16)
            result = jnp.dot(
                weights.reshape(2 * tokens, -1),
                listed(head, True, top_v),
                preferred_element_type=jnp.float32,
            )
            out_buf[g, :, :, head * head_width : (head + 1) * head_width] = result.reshape(
                2, tokens, head_width
            ).astype(jnp.bfloat16)
        pltpu.make_async_copy(out_buf.at[g], out.at[0, 0, :, :, at], out_sem).start()

    def step(t, _):
        @pl.when(t < chunks)
        def _():
            near_copy(t).wait_recv()

            @pl.when(has_to)
            def _():
                far_copy(t).start()

            sideways(NEAR, t)

        @pl.when(t + AHEAD < chunks)
        def _():
            send_own(t + AHEAD)

        @pl.when((t >= 1) & (t <= chunks) & has_far)
        def _():
            far_copy(t - 1).wait_recv()
            sideways(FAR, t - 1)

        @pl.when(t >= 2)
        def _():
            g = t - 2

            @pl.when(g == 0)
            def _():
                for s in range(1, cols):
                    top_copy(s).wait_recv()

            @pl.when(has_left)
            def _():
                to_right(OWN, g).wait_recv()
                to_right(NEAR, g).wait_recv()

            @pl.when(has_right)
            def _():
                to_left(OWN, g).wait_recv()
                to_left(NEAR, g).wait_recv()

            @pl.when(has_far & has_left)
            def _():
                to_right(FAR, g).wait_recv()

            @pl.when(has_far & has_right)
            def _():
                to_left(FAR, g).wait_recv()

            attend(g)

        return 0

    lax.fori_loop(0, chunks + 2, step, 0)

    remote(own.at[OWN], own.at[NEAR], near_send, near_recv.at[0], near_row, c).wait_send()

    @pl.when(has_to)
    def _():
        remote(own.at[NEAR], own.at[FAR], far_send, far_recv.at[0], far_to, c).wait_send()

    def sent(k):
        @pl.when(has_left)
        def _():
            remote(
                own.at[k, :, pl.ds(0, edge)],
                right.at[k],
                left_send.at[k],
                right_recv.at[k, 0],
                r,
                c - 1,
            ).wait_send()

        @pl.when(has_right)
        def _():
            remote(
                own.at[k, :, pl.ds(full - edge, edge)],
                left.at[k],
                right_send.at[k],
                left_recv.at[k, 0],
                r,
                c + 1,
            ).wait_send()

    sent(OWN)
    sent(NEAR)

    @pl.when(has_far)
    def _():
        sent(FAR)

    for s in range(1, cols):
        top_copy(s).wait_send()
    pltpu.make_async_copy(out_buf, out_buf, out_sem).wait()


def solution(mesh):
    row_count, col_count = mesh.shape["row"], mesh.shape["col"]

    def body(queries, keys, values, pool_keys, pool_values, top_keys, top_values, coarse_ids):
        tokens, model_width = queries.shape[3:]
        pool_blocks, pool_tokens, _ = pool_keys.shape
        pool_rows = pool_blocks * pool_tokens
        head_width = model_width // HEADS
        width = HEADS_PER_CHUNK * head_width
        chunks = model_width // width
        full = 4 * tokens + 2 * pool_rows
        edge = 2 * tokens + 2 * pool_rows
        per = top_keys.shape[1]
        listed = 3 * (4 * tokens + 3 * pool_rows) + col_count * per
        dims = (row_count, col_count, tokens, pool_rows, pool_blocks, chunks, width, head_width)
        dma = pltpu.SemaphoreType.DMA
        return pl.pallas_call(
            functools.partial(kernel, dims),
            out_shape=jax.ShapeDtypeStruct(queries.shape, queries.dtype),
            in_specs=[pl.BlockSpec(memory_space=pltpu.HBM)] * 8,
            out_specs=pl.BlockSpec(memory_space=pl.ANY),
            scratch_shapes=[
                pltpu.VMEM((3, chunks, full, width), jnp.bfloat16),
                pltpu.VMEM((3, chunks, edge, width), jnp.bfloat16),
                pltpu.VMEM((3, chunks, edge, width), jnp.bfloat16),
                pltpu.VMEM((2, tokens, model_width), jnp.bfloat16),
                pltpu.VMEM((chunks, 2, tokens, width), jnp.bfloat16),
                pltpu.VMEM((col_count, 2 * per, model_width), jnp.bfloat16),
                pltpu.VMEM((2, per, model_width), jnp.bfloat16),
                pltpu.SMEM(coarse_ids.shape, jnp.int32),
                pltpu.VMEM((2, listed), jnp.float32),
                dma((chunks,)),
                dma((2,)),
                dma,
                dma,
                dma,
                dma,
                dma((chunks,)),
                dma,
                dma((chunks,)),
                dma((3,)),
                dma((3, chunks)),
                dma((3,)),
                dma((3, chunks)),
                dma((col_count,)),
                dma((col_count,)),
            ],
            compiler_params=pltpu.CompilerParams(
                collective_id=0, has_side_effects=True, vmem_limit_bytes=63 * 2**20
            ),
            cost_estimate=pl.CostEstimate(
                flops=4 * 2 * tokens * listed * model_width,
                bytes_accessed=8 * 2**20,
                transcendentals=2 * tokens * listed * HEADS,
            ),
        )(queries, keys, values, pool_keys, pool_values, top_keys, top_values, coarse_ids)

    placed = (
        P(None, "row", "col", None, None),
        P(None, "row", "col", None, None),
        P(None, "row", "col", None, None),
        P(("row", "col"), None, None),
        P(("row", "col"), None, None),
        P(None, "col", None),
        P(None, "col", None),
        P(None, "row", "col", None),
    )
    return jax.shard_map(
        body,
        mesh=mesh,
        in_specs=placed,
        out_specs=P(None, "row", "col", None, None),
        check_vma=False,
    )
```

```python
import functools
import math

import jax
import jax.numpy as jnp
from jax import lax
from jax.experimental import pallas as pl
from jax.experimental.pallas import tpu as pltpu
from jax.sharding import PartitionSpec as P

HEADS = 16
NEG_FILL = -1e30
HEADS_PER_CHUNK = 1
AHEAD = 3
LOADS = 6
FAR_LAG = 2
ATTEND_LAG = 3
OWN, NEAR, FAR = 0, 1, 2


def kernel(
    dims,
    q_in,
    k_in,
    v_in,
    pk_in,
    pv_in,
    tk_in,
    tv_in,
    ids_in,
    out,
    own,
    left,
    right,
    q_buf,
    out_buf,
    top,
    top_own,
    ids,
    bias,
    load_sem,
    top_sem,
    ids_sem,
    q_sem,
    out_sem,
    near_send,
    near_recv,
    far_send,
    far_recv,
    left_send,
    left_recv,
    right_send,
    right_recv,
    top_send,
    top_recv,
):
    rows, cols, tokens, pool_rows, pool_blocks, chunks, width, head_width = dims
    pool_tokens = pool_rows // pool_blocks
    r = lax.axis_index("row")
    c = lax.axis_index("col")
    odd = lax.rem(r, 2)
    near_row = r + 1 - 2 * odd
    far_row = r - 1 + 2 * odd
    far_to = r + 2 - 4 * odd
    has_far = (far_row >= 0) & (far_row < rows)
    has_to = (far_to >= 0) & (far_to < rows)
    has_left = c > 0
    has_right = c < cols - 1
    low = 2 * tokens
    mid = low + 2 * pool_rows
    full = mid + 2 * tokens
    edge = mid

    def lanes(g):
        return pl.ds(pl.multiple_of(g * width, width), width)

    def load_chunk(g, _):
        at = lanes(g)
        pieces = (
            (k_in.at[0, 0, 0, :, at], 0, tokens),
            (v_in.at[0, 0, 0, :, at], tokens, tokens),
            (k_in.at[0, 0, 1, :, at], mid, tokens),
            (v_in.at[0, 0, 1, :, at], mid + tokens, tokens),
            (pk_in.at[:, at], low, pool_rows),
            (pv_in.at[:, at], low + pool_rows, pool_rows),
        )
        for source, start, size in pieces:
            pltpu.make_async_copy(
                source, own.at[OWN, g, pl.ds(start, size)], load_sem.at[g]
            ).start()
        return 0

    barrier = pltpu.get_barrier_semaphore()

    def greet(there, row, col):
        @pl.when(there)
        def _():
            pl.semaphore_signal(
                barrier, inc=1, device_id=(row, col), device_id_type=pl.DeviceIdType.MESH
            )

    pl.semaphore_signal(
        barrier, inc=1, device_id=(near_row, c), device_id_type=pl.DeviceIdType.MESH
    )
    greet(r + 2 < rows, r + 2, c)
    greet(r >= 2, r - 2, c)
    for step in range(1, cols):
        pl.semaphore_signal(
            barrier,
            inc=1,
            device_id=(r, lax.rem(c + step, cols)),
            device_id_type=pl.DeviceIdType.MESH,
        )

    lax.fori_loop(0, min(LOADS, chunks), load_chunk, 0)
    ids_copy = pltpu.make_async_copy(ids_in, ids, ids_sem)
    ids_copy.start()
    tk_copy = pltpu.make_async_copy(tk_in.at[0], top_own.at[0], top_sem.at[0])
    tk_copy.start()
    tv_copy = pltpu.make_async_copy(tv_in.at[0], top_own.at[1], top_sem.at[1])
    tv_copy.start()
    q_copy = pltpu.make_async_copy(q_in.at[0, 0], q_buf, q_sem)
    q_copy.start()

    greeted = (
        1
        + (r + 2 < rows).astype(jnp.int32)
        + (r >= 2).astype(jnp.int32)
        + (cols - 1)
    )
    pl.semaphore_wait(barrier, greeted)

    def remote(source, target, send, recv, row, col):
        return pltpu.make_async_remote_copy(
            src_ref=source,
            dst_ref=target,
            send_sem=send,
            recv_sem=recv,
            device_id=(row, col),
            device_id_type=pl.DeviceIdType.MESH,
        )

    def near_copy(g):
        return remote(
            own.at[OWN, g], own.at[NEAR, g], near_send, near_recv.at[g], near_row, c
        )

    def far_copy(g):
        return remote(own.at[NEAR, g], own.at[FAR, g], far_send, far_recv.at[g], far_to, c)

    def to_left(k, g):
        return remote(
            own.at[k, g, pl.ds(0, edge)],
            right.at[k, g],
            left_send.at[k],
            right_recv.at[k, g],
            r,
            c - 1,
        )

    def to_right(k, g):
        return remote(
            own.at[k, g, pl.ds(full - edge, edge)],
            left.at[k, g],
            right_send.at[k],
            left_recv.at[k, g],
            r,
            c + 1,
        )

    def sideways(k, g):
        @pl.when(has_left)
        def _():
            to_left(k, g).start()

        @pl.when(has_right)
        def _():
            to_right(k, g).start()

    def top_copy(step):
        to = lax.rem(c + step, cols)
        return remote(top.at[c], top.at[c], top_send.at[step], top_recv.at[step], r, to)

    def send_own(g):
        pltpu.make_async_copy(own.at[OWN, g], own.at[OWN, g], load_sem.at[g]).wait()
        near_copy(g).start()
        sideways(OWN, g)

    for g in range(min(AHEAD, chunks)):
        send_own(g)
    tk_copy.wait()
    tv_copy.wait()
    ids_copy.wait()
    top[c] = jnp.concatenate(
        [top_own[0].astype(jnp.float32), top_own[1].astype(jnp.float32)], axis=0
    ).astype(jnp.bfloat16)

    for step in range(1, cols):
        top_copy(step).start()

    @pl.when(jnp.logical_not(has_far))
    def _():
        own[FAR] = jnp.zeros(own.shape[1:], own.dtype)

    @pl.when(jnp.logical_not(has_far & has_left))
    def _():
        left[FAR] = jnp.zeros(left.shape[1:], left.dtype)

    @pl.when(jnp.logical_not(has_far & has_right))
    def _():
        right[FAR] = jnp.zeros(right.shape[1:], right.dtype)

    @pl.when(jnp.logical_not(has_left))
    def _():
        for k in (OWN, NEAR):
            left[k] = jnp.zeros(left.shape[1:], left.dtype)

    @pl.when(jnp.logical_not(has_right))
    def _():
        for k in (OWN, NEAR):
            right[k] = jnp.zeros(right.shape[1:], right.dtype)

    top_rows = cols * tk_in.shape[1]
    for b in range(2):
        parts = []
        for k, row in ((OWN, r), (NEAR, near_row), (FAR, far_row)):
            row_there = (row >= 0) & (row < rows)
            for slot in range(4):
                if slot in (b, b + 1, b + 2):
                    there = row_there
                    if slot == 0:
                        there = there & has_left
                    if slot == 3:
                        there = there & has_right
                    value = jnp.where(there, 0.0, NEG_FILL)
                else:
                    value = jnp.float32(NEG_FILL)
                parts.append(jnp.full((1, tokens), value, jnp.float32))
            for shift in (-1, 0, 1):
                there = row_there & (c + shift >= 0) & (c + shift < cols)
                base = (row * cols + c + shift) * pool_blocks
                for block in range(pool_blocks):
                    listed_here = jnp.int32(0)
                    for n in range(ids.shape[3]):
                        listed_here = listed_here | (ids[0, 0, b, n] == base + block).astype(
                            jnp.int32
                        )
                    listed_here = listed_here * there.astype(jnp.int32)
                    value = (1.0 - listed_here.astype(jnp.float32)) * NEG_FILL
                    parts.append(jnp.full((1, pool_tokens), value, jnp.float32))
        parts.append(jnp.zeros((1, top_rows), jnp.float32))
        at = 0
        for part in parts:
            bias[b : b + 1, at : at + part.shape[1]] = part
            at += part.shape[1]

    q_copy.wait()

    score_scale = math.log2(math.e) / math.sqrt(head_width)

    def attend(g):
        at = lanes(g)
        q_chunk = q_buf[:, :, at].reshape(2 * tokens, width)
        tops = top[:, :, at].astype(jnp.float32)
        per = tk_in.shape[1]
        top_k = tops[:, :per].reshape(top_rows, width).astype(jnp.bfloat16)
        top_v = tops[:, per:].reshape(top_rows, width).astype(jnp.bfloat16)

        def listed(head, value, top_part):
            lane = pl.ds(head * head_width, head_width)
            fine = tokens if value else 0
            pool = pool_rows if value else 0
            side = full - edge
            parts = []
            for k in (OWN, NEAR, FAR):
                parts += [
                    left[k, g, pl.ds(mid + fine - side, tokens), lane],
                    own[k, g, pl.ds(fine, tokens), lane],
                    own[k, g, pl.ds(mid + fine, tokens), lane],
                    right[k, g, pl.ds(fine, tokens), lane],
                    left[k, g, pl.ds(low + pool - side, pool_rows), lane],
                    own[k, g, pl.ds(low + pool, pool_rows), lane],
                    right[k, g, pl.ds(low + pool, pool_rows), lane],
                ]
            parts.append(top_part[:, head * head_width : (head + 1) * head_width])
            return jnp.concatenate(parts, axis=0)

        for head in range(width // head_width):
            q_head = q_chunk[:, head * head_width : (head + 1) * head_width]
            scores = lax.dot_general(
                q_head,
                listed(head, False, top_k),
                (((1,), (1,)), ((), ())),
                preferred_element_type=jnp.float32,
            )
            scores = (scores * score_scale).reshape(2, tokens, -1) + bias[...][:, None, :]
            peak = jnp.max(scores, axis=-1, keepdims=True)
            exponent = jnp.exp2(scores - peak)
            total = jnp.sum(exponent, axis=-1, keepdims=True)
            weights = (exponent * (1.0 / total)).astype(jnp.bfloat16)
            result = jnp.dot(
                weights.reshape(2 * tokens, -1),
                listed(head, True, top_v),
                preferred_element_type=jnp.float32,
            )
            out_buf[g, :, :, head * head_width : (head + 1) * head_width] = result.reshape(
                2, tokens, head_width
            ).astype(jnp.bfloat16)
        pltpu.make_async_copy(out_buf.at[g], out.at[0, 0, :, :, at], out_sem).start()

    def step(t, _):
        @pl.when(t < chunks)
        def _():
            near_copy(t).wait_recv()

            @pl.when(has_to)
            def _():
                far_copy(t).start()

            sideways(NEAR, t)

        @pl.when(t + AHEAD < chunks)
        def _():
            send_own(t + AHEAD)

        @pl.when(t + LOADS < chunks)
        def _():
            load_chunk(t + LOADS, 0)

        @pl.when((t >= FAR_LAG) & (t < chunks + FAR_LAG) & has_far)
        def _():
            far_copy(t - FAR_LAG).wait_recv()
            sideways(FAR, t - FAR_LAG)

        @pl.when(t >= ATTEND_LAG)
        def _():
            g = t - ATTEND_LAG

            @pl.when(g == 0)
            def _():
                for s in range(1, cols):
                    top_copy(s).wait_recv()

            @pl.when(has_left)
            def _():
                to_right(OWN, g).wait_recv()
                to_right(NEAR, g).wait_recv()

            @pl.when(has_right)
            def _():
                to_left(OWN, g).wait_recv()
                to_left(NEAR, g).wait_recv()

            @pl.when(has_far & has_left)
            def _():
                to_right(FAR, g).wait_recv()

            @pl.when(has_far & has_right)
            def _():
                to_left(FAR, g).wait_recv()

            attend(g)

        return 0

    lax.fori_loop(0, chunks + ATTEND_LAG, step, 0)

    remote(own.at[OWN], own.at[NEAR], near_send, near_recv.at[0], near_row, c).wait_send()

    @pl.when(has_to)
    def _():
        remote(own.at[NEAR], own.at[FAR], far_send, far_recv.at[0], far_to, c).wait_send()

    def sent(k):
        @pl.when(has_left)
        def _():
            remote(
                own.at[k, :, pl.ds(0, edge)],
                right.at[k],
                left_send.at[k],
                right_recv.at[k, 0],
                r,
                c - 1,
            ).wait_send()

        @pl.when(has_right)
        def _():
            remote(
                own.at[k, :, pl.ds(full - edge, edge)],
                left.at[k],
                right_send.at[k],
                left_recv.at[k, 0],
                r,
                c + 1,
            ).wait_send()

    sent(OWN)
    sent(NEAR)

    @pl.when(has_far)
    def _():
        sent(FAR)

    for s in range(1, cols):
        top_copy(s).wait_send()
    pltpu.make_async_copy(out_buf, out_buf, out_sem).wait()


def solution(mesh):
    row_count, col_count = mesh.shape["row"], mesh.shape["col"]

    def body(queries, keys, values, pool_keys, pool_values, top_keys, top_values, coarse_ids):
        tokens, model_width = queries.shape[3:]
        pool_blocks, pool_tokens, _ = pool_keys.shape
        pool_rows = pool_blocks * pool_tokens
        head_width = model_width // HEADS
        width = HEADS_PER_CHUNK * head_width
        chunks = model_width // width
        full = 4 * tokens + 2 * pool_rows
        edge = 2 * tokens + 2 * pool_rows
        per = top_keys.shape[1]
        listed = 3 * (4 * tokens + 3 * pool_rows) + col_count * per
        dims = (row_count, col_count, tokens, pool_rows, pool_blocks, chunks, width, head_width)
        dma = pltpu.SemaphoreType.DMA
        return pl.pallas_call(
            functools.partial(kernel, dims),
            out_shape=jax.ShapeDtypeStruct(queries.shape, queries.dtype),
            in_specs=[pl.BlockSpec(memory_space=pltpu.HBM)] * 8,
            out_specs=pl.BlockSpec(memory_space=pl.ANY),
            scratch_shapes=[
                pltpu.VMEM((3, chunks, full, width), jnp.bfloat16),
                pltpu.VMEM((3, chunks, edge, width), jnp.bfloat16),
                pltpu.VMEM((3, chunks, edge, width), jnp.bfloat16),
                pltpu.VMEM((2, tokens, model_width), jnp.bfloat16),
                pltpu.VMEM((chunks, 2, tokens, width), jnp.bfloat16),
                pltpu.VMEM((col_count, 2 * per, model_width), jnp.bfloat16),
                pltpu.VMEM((2, per, model_width), jnp.bfloat16),
                pltpu.SMEM(coarse_ids.shape, jnp.int32),
                pltpu.VMEM((2, listed), jnp.float32),
                dma((chunks,)),
                dma((2,)),
                dma,
                dma,
                dma,
                dma,
                dma((chunks,)),
                dma,
                dma((chunks,)),
                dma((3,)),
                dma((3, chunks)),
                dma((3,)),
                dma((3, chunks)),
                dma((col_count,)),
                dma((col_count,)),
            ],
            compiler_params=pltpu.CompilerParams(
                collective_id=0, has_side_effects=True, vmem_limit_bytes=63 * 2**20
            ),
            cost_estimate=pl.CostEstimate(
                flops=4 * 2 * tokens * listed * model_width,
                bytes_accessed=8 * 2**20,
                transcendentals=2 * tokens * listed * HEADS,
            ),
        )(
            queries,
            keys,
            values,
            pool_keys.reshape(pool_rows, model_width),
            pool_values.reshape(pool_rows, model_width),
            top_keys,
            top_values,
            coarse_ids,
        )

    placed = (
        P(None, "row", "col", None, None),
        P(None, "row", "col", None, None),
        P(None, "row", "col", None, None),
        P(("row", "col"), None, None),
        P(("row", "col"), None, None),
        P(None, "col", None),
        P(None, "col", None),
        P(None, "row", "col", None),
    )
    return jax.shard_map(
        body,
        mesh=mesh,
        in_specs=placed,
        out_specs=P(None, "row", "col", None, None),
        check_vma=False,
    )
```

```python
import functools
import math

import jax
import jax.numpy as jnp
from jax import lax
from jax.experimental import pallas as pl
from jax.experimental.pallas import tpu as pltpu
from jax.sharding import PartitionSpec as P

HEADS = 16
NEG_FILL = -1e30
HEADS_PER_CHUNK = 2
AHEAD = 3
LOADS = 5
FAR_LAG = 1
ATTEND_LAG = 3
OWN, NEAR, FAR = 0, 1, 2


def kernel(
    dims,
    q_in,
    k_in,
    v_in,
    pk_in,
    pv_in,
    tk_in,
    tv_in,
    ids_in,
    out,
    own,
    left,
    right,
    q_buf,
    out_buf,
    top,
    top_own,
    ids,
    bias,
    load_sem,
    top_sem,
    ids_sem,
    q_sem,
    out_sem,
    near_send,
    near_recv,
    far_send,
    far_recv,
    left_send,
    left_recv,
    right_send,
    right_recv,
    top_send,
    top_recv,
):
    rows, cols, tokens, pool_rows, pool_blocks, chunks, width, head_width = dims
    pool_tokens = pool_rows // pool_blocks
    r = lax.axis_index("row")
    c = lax.axis_index("col")
    odd = lax.rem(r, 2)
    near_row = r + 1 - 2 * odd
    far_row = r - 1 + 2 * odd
    far_to = r + 2 - 4 * odd
    has_far = (far_row >= 0) & (far_row < rows)
    has_to = (far_to >= 0) & (far_to < rows)
    has_left = c > 0
    has_right = c < cols - 1
    low = 2 * tokens
    mid = low + 2 * pool_rows
    full = mid + 2 * tokens
    edge = mid

    def lanes(g):
        return pl.ds(pl.multiple_of(g * width, width), width)

    def load_chunk(g, _):
        at = lanes(g)
        pieces = (
            (k_in.at[0, 0, 0, :, at], 0, tokens),
            (v_in.at[0, 0, 0, :, at], tokens, tokens),
            (k_in.at[0, 0, 1, :, at], mid, tokens),
            (v_in.at[0, 0, 1, :, at], mid + tokens, tokens),
            (pk_in.at[:, at], low, pool_rows),
            (pv_in.at[:, at], low + pool_rows, pool_rows),
        )
        for source, start, size in pieces:
            pltpu.make_async_copy(
                source, own.at[OWN, g, pl.ds(start, size)], load_sem.at[g]
            ).start()
        return 0

    barrier = pltpu.get_barrier_semaphore()

    def greet(there, row, col):
        @pl.when(there)
        def _():
            pl.semaphore_signal(
                barrier, inc=1, device_id=(row, col), device_id_type=pl.DeviceIdType.MESH
            )

    pl.semaphore_signal(
        barrier, inc=1, device_id=(near_row, c), device_id_type=pl.DeviceIdType.MESH
    )
    greet(r + 2 < rows, r + 2, c)
    greet(r >= 2, r - 2, c)
    for step in range(1, cols):
        pl.semaphore_signal(
            barrier,
            inc=1,
            device_id=(r, lax.rem(c + step, cols)),
            device_id_type=pl.DeviceIdType.MESH,
        )

    lax.fori_loop(0, min(LOADS, chunks), load_chunk, 0)
    ids_copy = pltpu.make_async_copy(ids_in, ids, ids_sem)
    ids_copy.start()
    tk_copy = pltpu.make_async_copy(tk_in.at[0], top_own.at[0], top_sem.at[0])
    tk_copy.start()
    tv_copy = pltpu.make_async_copy(tv_in.at[0], top_own.at[1], top_sem.at[1])
    tv_copy.start()
    q_copy = pltpu.make_async_copy(q_in.at[0, 0], q_buf, q_sem)
    q_copy.start()

    greeted = (
        1
        + (r + 2 < rows).astype(jnp.int32)
        + (r >= 2).astype(jnp.int32)
        + (cols - 1)
    )
    pl.semaphore_wait(barrier, greeted)

    def remote(source, target, send, recv, row, col):
        return pltpu.make_async_remote_copy(
            src_ref=source,
            dst_ref=target,
            send_sem=send,
            recv_sem=recv,
            device_id=(row, col),
            device_id_type=pl.DeviceIdType.MESH,
        )

    def near_copy(g):
        return remote(
            own.at[OWN, g], own.at[NEAR, g], near_send, near_recv.at[g], near_row, c
        )

    def far_copy(g):
        return remote(own.at[NEAR, g], own.at[FAR, g], far_send, far_recv.at[g], far_to, c)

    def to_left(k, g):
        return remote(
            own.at[k, g, pl.ds(0, edge)],
            right.at[k, g],
            left_send.at[k],
            right_recv.at[k, g],
            r,
            c - 1,
        )

    def to_right(k, g):
        return remote(
            own.at[k, g, pl.ds(full - edge, edge)],
            left.at[k, g],
            right_send.at[k],
            left_recv.at[k, g],
            r,
            c + 1,
        )

    def sideways(k, g):
        @pl.when(has_left)
        def _():
            to_left(k, g).start()

        @pl.when(has_right)
        def _():
            to_right(k, g).start()

    def top_copy(step):
        to = lax.rem(c + step, cols)
        return remote(top.at[c], top.at[c], top_send.at[step], top_recv.at[step], r, to)

    def send_own(g):
        pltpu.make_async_copy(own.at[OWN, g], own.at[OWN, g], load_sem.at[g]).wait()
        near_copy(g).start()
        sideways(OWN, g)

    for g in range(min(AHEAD, chunks)):
        send_own(g)
    tk_copy.wait()
    tv_copy.wait()
    ids_copy.wait()
    top[c] = jnp.concatenate(
        [top_own[0].astype(jnp.float32), top_own[1].astype(jnp.float32)], axis=0
    ).astype(jnp.bfloat16)

    for step in range(1, cols):
        top_copy(step).start()

    @pl.when(jnp.logical_not(has_far))
    def _():
        own[FAR] = jnp.zeros(own.shape[1:], own.dtype)

    @pl.when(jnp.logical_not(has_far & has_left))
    def _():
        left[FAR] = jnp.zeros(left.shape[1:], left.dtype)

    @pl.when(jnp.logical_not(has_far & has_right))
    def _():
        right[FAR] = jnp.zeros(right.shape[1:], right.dtype)

    @pl.when(jnp.logical_not(has_left))
    def _():
        for k in (OWN, NEAR):
            left[k] = jnp.zeros(left.shape[1:], left.dtype)

    @pl.when(jnp.logical_not(has_right))
    def _():
        for k in (OWN, NEAR):
            right[k] = jnp.zeros(right.shape[1:], right.dtype)

    top_rows = cols * tk_in.shape[1]
    for b in range(2):
        parts = []
        for k, row in ((OWN, r), (NEAR, near_row), (FAR, far_row)):
            row_there = (row >= 0) & (row < rows)
            for slot in range(4):
                if slot in (b, b + 1, b + 2):
                    there = row_there
                    if slot == 0:
                        there = there & has_left
                    if slot == 3:
                        there = there & has_right
                    value = jnp.where(there, 0.0, NEG_FILL)
                else:
                    value = jnp.float32(NEG_FILL)
                parts.append(jnp.full((1, tokens), value, jnp.float32))
            for shift in (-1, 0, 1):
                there = row_there & (c + shift >= 0) & (c + shift < cols)
                base = (row * cols + c + shift) * pool_blocks
                for block in range(pool_blocks):
                    listed_here = jnp.int32(0)
                    for n in range(ids.shape[3]):
                        listed_here = listed_here | (ids[0, 0, b, n] == base + block).astype(
                            jnp.int32
                        )
                    listed_here = listed_here * there.astype(jnp.int32)
                    value = (1.0 - listed_here.astype(jnp.float32)) * NEG_FILL
                    parts.append(jnp.full((1, pool_tokens), value, jnp.float32))
        parts.append(jnp.zeros((1, top_rows), jnp.float32))
        at = 0
        for part in parts:
            bias[b : b + 1, at : at + part.shape[1]] = part
            at += part.shape[1]

    q_copy.wait()

    score_scale = math.log2(math.e) / math.sqrt(head_width)

    def attend(g):
        at = lanes(g)
        q_chunk = q_buf[:, :, at].reshape(2 * tokens, width)
        tops = top[:, :, at].astype(jnp.float32)
        per = tk_in.shape[1]
        top_k = tops[:, :per].reshape(top_rows, width).astype(jnp.bfloat16)
        top_v = tops[:, per:].reshape(top_rows, width).astype(jnp.bfloat16)

        def listed(head, value, top_part):
            lane = pl.ds(head * head_width, head_width)
            fine = tokens if value else 0
            pool = pool_rows if value else 0
            side = full - edge
            parts = []
            for k in (OWN, NEAR, FAR):
                parts += [
                    left[k, g, pl.ds(mid + fine - side, tokens), lane],
                    own[k, g, pl.ds(fine, tokens), lane],
                    own[k, g, pl.ds(mid + fine, tokens), lane],
                    right[k, g, pl.ds(fine, tokens), lane],
                    left[k, g, pl.ds(low + pool - side, pool_rows), lane],
                    own[k, g, pl.ds(low + pool, pool_rows), lane],
                    right[k, g, pl.ds(low + pool, pool_rows), lane],
                ]
            parts.append(top_part[:, head * head_width : (head + 1) * head_width])
            return jnp.concatenate(parts, axis=0)

        for head in range(width // head_width):
            q_head = q_chunk[:, head * head_width : (head + 1) * head_width]
            scores = lax.dot_general(
                q_head,
                listed(head, False, top_k),
                (((1,), (1,)), ((), ())),
                preferred_element_type=jnp.float32,
            )
            scores = (scores * score_scale).reshape(2, tokens, -1) + bias[...][:, None, :]
            peak = jnp.max(scores, axis=-1, keepdims=True)
            exponent = jnp.exp2(scores - peak)
            total = jnp.sum(exponent, axis=-1, keepdims=True)
            weights = (exponent * (1.0 / total)).astype(jnp.bfloat16)
            result = jnp.dot(
                weights.reshape(2 * tokens, -1),
                listed(head, True, top_v),
                preferred_element_type=jnp.float32,
            )
            out_buf[g, :, :, head * head_width : (head + 1) * head_width] = result.reshape(
                2, tokens, head_width
            ).astype(jnp.bfloat16)
        pltpu.make_async_copy(out_buf.at[g], out.at[0, 0, :, :, at], out_sem).start()

    def step(t, _):
        @pl.when(t < chunks)
        def _():
            near_copy(t).wait_recv()

            @pl.when(has_to)
            def _():
                far_copy(t).start()

            sideways(NEAR, t)

        @pl.when(t + AHEAD < chunks)
        def _():
            send_own(t + AHEAD)

        @pl.when(t + LOADS < chunks)
        def _():
            load_chunk(t + LOADS, 0)

        @pl.when(t >= ATTEND_LAG)
        def _():
            g = t - ATTEND_LAG

            @pl.when(g == 0)
            def _():
                for s in range(1, cols):
                    top_copy(s).wait_recv()

            @pl.when(has_left)
            def _():
                to_right(OWN, g).wait_recv()
                to_right(NEAR, g).wait_recv()

            @pl.when(has_right)
            def _():
                to_left(OWN, g).wait_recv()
                to_left(NEAR, g).wait_recv()

            @pl.when(has_far & has_left)
            def _():
                to_right(FAR, g).wait_recv()

            @pl.when(has_far & has_right)
            def _():
                to_left(FAR, g).wait_recv()

            attend(g)

        @pl.when((t >= FAR_LAG) & (t < chunks + FAR_LAG) & has_far)
        def _():
            far_copy(t - FAR_LAG).wait_recv()
            sideways(FAR, t - FAR_LAG)

        return 0

    lax.fori_loop(0, chunks + ATTEND_LAG, step, 0)

    remote(own.at[OWN], own.at[NEAR], near_send, near_recv.at[0], near_row, c).wait_send()

    @pl.when(has_to)
    def _():
        remote(own.at[NEAR], own.at[FAR], far_send, far_recv.at[0], far_to, c).wait_send()

    def sent(k):
        @pl.when(has_left)
        def _():
            remote(
                own.at[k, :, pl.ds(0, edge)],
                right.at[k],
                left_send.at[k],
                right_recv.at[k, 0],
                r,
                c - 1,
            ).wait_send()

        @pl.when(has_right)
        def _():
            remote(
                own.at[k, :, pl.ds(full - edge, edge)],
                left.at[k],
                right_send.at[k],
                left_recv.at[k, 0],
                r,
                c + 1,
            ).wait_send()

    sent(OWN)
    sent(NEAR)

    @pl.when(has_far)
    def _():
        sent(FAR)

    for s in range(1, cols):
        top_copy(s).wait_send()
    pltpu.make_async_copy(out_buf, out_buf, out_sem).wait()


def solution(mesh):
    row_count, col_count = mesh.shape["row"], mesh.shape["col"]

    def body(queries, keys, values, pool_keys, pool_values, top_keys, top_values, coarse_ids):
        tokens, model_width = queries.shape[3:]
        pool_blocks, pool_tokens, _ = pool_keys.shape
        pool_rows = pool_blocks * pool_tokens
        head_width = model_width // HEADS
        width = HEADS_PER_CHUNK * head_width
        chunks = model_width // width
        full = 4 * tokens + 2 * pool_rows
        edge = 2 * tokens + 2 * pool_rows
        per = top_keys.shape[1]
        listed = 3 * (4 * tokens + 3 * pool_rows) + col_count * per
        dims = (row_count, col_count, tokens, pool_rows, pool_blocks, chunks, width, head_width)
        dma = pltpu.SemaphoreType.DMA
        return pl.pallas_call(
            functools.partial(kernel, dims),
            out_shape=jax.ShapeDtypeStruct(queries.shape, queries.dtype),
            in_specs=[pl.BlockSpec(memory_space=pltpu.HBM)] * 8,
            out_specs=pl.BlockSpec(memory_space=pl.ANY),
            scratch_shapes=[
                pltpu.VMEM((3, chunks, full, width), jnp.bfloat16),
                pltpu.VMEM((3, chunks, edge, width), jnp.bfloat16),
                pltpu.VMEM((3, chunks, edge, width), jnp.bfloat16),
                pltpu.VMEM((2, tokens, model_width), jnp.bfloat16),
                pltpu.VMEM((chunks, 2, tokens, width), jnp.bfloat16),
                pltpu.VMEM((col_count, 2 * per, model_width), jnp.bfloat16),
                pltpu.VMEM((2, per, model_width), jnp.bfloat16),
                pltpu.SMEM(coarse_ids.shape, jnp.int32),
                pltpu.VMEM((2, listed), jnp.float32),
                dma((chunks,)),
                dma((2,)),
                dma,
                dma,
                dma,
                dma,
                dma((chunks,)),
                dma,
                dma((chunks,)),
                dma((3,)),
                dma((3, chunks)),
                dma((3,)),
                dma((3, chunks)),
                dma((col_count,)),
                dma((col_count,)),
            ],
            compiler_params=pltpu.CompilerParams(
                collective_id=0, has_side_effects=True, vmem_limit_bytes=63 * 2**20
            ),
            cost_estimate=pl.CostEstimate(
                flops=4 * 2 * tokens * listed * model_width,
                bytes_accessed=8 * 2**20,
                transcendentals=2 * tokens * listed * HEADS,
            ),
        )(
            queries,
            keys,
            values,
            pool_keys.reshape(pool_rows, model_width),
            pool_values.reshape(pool_rows, model_width),
            top_keys,
            top_values,
            coarse_ids,
        )

    placed = (
        P(None, "row", "col", None, None),
        P(None, "row", "col", None, None),
        P(None, "row", "col", None, None),
        P(("row", "col"), None, None),
        P(("row", "col"), None, None),
        P(None, "col", None),
        P(None, "col", None),
        P(None, "row", "col", None),
    )
    return jax.shard_map(
        body,
        mesh=mesh,
        in_specs=placed,
        out_specs=P(None, "row", "col", None, None),
        check_vma=False,
    )
```

```python
import functools
import math

import jax
import jax.numpy as jnp
from jax import lax
from jax.experimental import pallas as pl
from jax.experimental.pallas import tpu as pltpu
from jax.sharding import PartitionSpec as P

HEADS = 16
NEG_FILL = -1e30
AHEAD = 2
LOADS = 3
FAR_LAG = 1
ATTEND_LAG = 2
MINE, MATE, BY_MINE, BY_MATE = range(4)


def kernel(
    dims,
    q_in,
    k_in,
    v_in,
    pk_in,
    pv_in,
    tk_in,
    tv_in,
    ids_in,
    out,
    own,
    give,
    left,
    right,
    back,
    top,
    top_own,
    ids,
    bias,
    load_sem,
    give_load_sem,
    top_sem,
    ids_sem,
    give_send,
    mate_recv,
    by_mine_send,
    by_mine_recv,
    by_mate_send,
    by_mate_recv,
    left_send,
    left_recv,
    right_send,
    right_recv,
    top_send,
    top_recv,
    bias_send,
    bias_recv,
    back_send,
    back_recv,
):
    rows, cols, tokens, pool_rows, pool_blocks, heads, width, listed_count = dims
    pool_tokens = pool_rows // pool_blocks
    r = lax.axis_index("row")
    c = lax.axis_index("col")
    odd = lax.rem(r, 2)
    mate = r + 1 - 2 * odd
    mine_to = r - 2 + 4 * odd
    mate_to = r + 2 - 4 * odd
    by_mine_row = r - 1 + 2 * odd
    has_by_mine = (mine_to >= 0) & (mine_to < rows)
    has_by_mate = (mate_to >= 0) & (mate_to < rows)
    has_left = c > 0
    has_right = c < cols - 1
    low = 2 * tokens
    mid = low + 2 * pool_rows
    full = mid + 2 * tokens
    edge = mid
    whole = full + 2 * tokens

    def lanes(half, h):
        return pl.ds(pl.multiple_of((half * heads + h) * width, width), width)

    def load_tile(half, h, tile, sem):
        at = lanes(half, h)
        pieces = (
            (k_in.at[pl.ds(0, tokens), at], 0, tokens),
            (v_in.at[pl.ds(0, tokens), at], tokens, tokens),
            (pk_in.at[:, at], low, pool_rows),
            (pv_in.at[:, at], low + pool_rows, pool_rows),
            (k_in.at[pl.ds(tokens, tokens), at], mid, tokens),
            (v_in.at[pl.ds(tokens, tokens), at], mid + tokens, tokens),
            (q_in.at[:, at], full, 2 * tokens),
        )
        for source, start, size in pieces:
            pltpu.make_async_copy(source, tile.at[pl.ds(start, size)], sem).start()

    def load(h):
        load_tile(1 - odd, h, give.at[h], give_load_sem.at[h])
        load_tile(odd, h, own.at[MINE, h], load_sem.at[h])

    barrier = pltpu.get_barrier_semaphore()

    def signal(row, col):
        pl.semaphore_signal(
            barrier, inc=1, device_id=(row, col), device_id_type=pl.DeviceIdType.MESH
        )

    signal(mate, c)

    @pl.when(r + 2 < rows)
    def _():
        signal(r + 2, c)

    @pl.when(r >= 2)
    def _():
        signal(r - 2, c)

    for step in range(1, cols):
        signal(r, lax.rem(c + step, cols))

    load(0)
    ids_copy = pltpu.make_async_copy(ids_in, ids, ids_sem)
    ids_copy.start()
    half_lanes = pl.ds(pl.multiple_of(odd * heads * width, heads * width), heads * width)
    tk_copy = pltpu.make_async_copy(tk_in.at[0, :, half_lanes], top_own.at[0], top_sem.at[0])
    tk_copy.start()
    tv_copy = pltpu.make_async_copy(tv_in.at[0, :, half_lanes], top_own.at[1], top_sem.at[1])
    tv_copy.start()
    for h in range(1, min(LOADS, heads)):
        load(h)

    greeted = 1 + (r + 2 < rows).astype(jnp.int32) + (r >= 2).astype(jnp.int32) + (cols - 1)
    pl.semaphore_wait(barrier, greeted)

    def remote(source, target, send, recv, row, col):
        return pltpu.make_async_remote_copy(
            src_ref=source,
            dst_ref=target,
            send_sem=send,
            recv_sem=recv,
            device_id=(row, col),
            device_id_type=pl.DeviceIdType.MESH,
        )

    def give_copy(h):
        return remote(give.at[h], own.at[MATE, h], give_send, mate_recv.at[h], mate, c)

    def by_mine_copy(h):
        return remote(
            own.at[MATE, h, pl.ds(0, full)],
            own.at[BY_MINE, h, pl.ds(0, full)],
            by_mine_send,
            by_mine_recv.at[h],
            mate_to,
            c,
        )

    def by_mate_copy(h):
        return remote(
            own.at[MINE, h, pl.ds(0, full)],
            own.at[BY_MATE, h, pl.ds(0, full)],
            by_mate_send,
            by_mate_recv.at[h],
            mine_to,
            c,
        )

    def to_left(k, h):
        return remote(
            own.at[k, h, pl.ds(0, edge)],
            right.at[k, h],
            left_send.at[k],
            right_recv.at[k, h],
            r,
            c - 1,
        )

    def to_right(k, h):
        return remote(
            own.at[k, h, pl.ds(full - edge, edge)],
            left.at[k, h],
            right_send.at[k],
            left_recv.at[k, h],
            r,
            c + 1,
        )

    def sideways(k, h):
        @pl.when(has_left)
        def _():
            to_left(k, h).start()

        @pl.when(has_right)
        def _():
            to_right(k, h).start()

    def top_copy(step):
        to = lax.rem(c + step, cols)
        return remote(top.at[c], top.at[c], top_send.at[step], top_recv.at[step], r, to)

    def back_copy(h):
        return remote(
            back.at[h], out.at[0, 0, :, :, lanes(odd, h)], back_send, back_recv, mate, c
        )

    bias_copy = remote(bias.at[MINE], bias.at[MATE], bias_send, bias_recv, mate, c)

    def send_own(h):
        pltpu.make_async_copy(give.at[h], give.at[h], give_load_sem.at[h]).wait()
        give_copy(h).start()
        pltpu.make_async_copy(own.at[MINE, h], own.at[MINE, h], load_sem.at[h]).wait()

        @pl.when(has_by_mine)
        def _():
            by_mate_copy(h).start()

        sideways(MINE, h)

    for h in range(min(AHEAD, heads)):
        send_own(h)
    tk_copy.wait()
    tv_copy.wait()
    ids_copy.wait()
    top[c] = jnp.concatenate(
        [top_own[0].astype(jnp.float32), top_own[1].astype(jnp.float32)], axis=0
    ).astype(jnp.bfloat16)
    for step in range(1, cols):
        top_copy(step).start()

    per = tk_in.shape[1]
    top_rows = cols * per
    for b in range(2):
        parts = []
        for row, row_there in ((r, True), (mate, True), (by_mine_row, has_by_mine)):
            for slot in range(4):
                if slot in (b, b + 1, b + 2):
                    there = jnp.logical_and(row_there, True)
                    if slot == 0:
                        there = there & has_left
                    if slot == 3:
                        there = there & has_right
                    value = jnp.where(there, 0.0, NEG_FILL)
                else:
                    value = jnp.float32(NEG_FILL)
                parts.append(jnp.full((1, tokens), value, jnp.float32))
            for shift in (-1, 0, 1):
                there = jnp.logical_and(row_there, (c + shift >= 0) & (c + shift < cols))
                base = (row * cols + c + shift) * pool_blocks
                for block in range(pool_blocks):
                    here = jnp.int32(0)
                    for n in range(ids.shape[3]):
                        here = here | (ids[0, 0, b, n] == base + block).astype(jnp.int32)
                    here = here * there.astype(jnp.int32)
                    value = (1.0 - here.astype(jnp.float32)) * NEG_FILL
                    parts.append(jnp.full((1, pool_tokens), value, jnp.float32))
        parts.append(jnp.zeros((1, top_rows), jnp.float32))
        at = 0
        for part in parts:
            bias[MINE, b : b + 1, at : at + part.shape[1]] = part
            at += part.shape[1]
    bias_copy.start()

    def clear(there, k):
        @pl.when(jnp.logical_not(there))
        def _():
            own[k, :, pl.ds(0, full)] = jnp.zeros((heads, full, width), own.dtype)

        @pl.when(jnp.logical_not(there & has_left))
        def _():
            left[k] = jnp.zeros(left.shape[1:], left.dtype)

        @pl.when(jnp.logical_not(there & has_right))
        def _():
            right[k] = jnp.zeros(right.shape[1:], right.dtype)

    for k in (MINE, MATE):
        @pl.when(jnp.logical_not(has_left))
        def _():
            left[k] = jnp.zeros(left.shape[1:], left.dtype)

        @pl.when(jnp.logical_not(has_right))
        def _():
            right[k] = jnp.zeros(right.shape[1:], right.dtype)

    clear(has_by_mine, BY_MINE)
    clear(has_by_mate, BY_MATE)

    score_scale = math.log2(math.e) / math.sqrt(width)

    def attend(h):
        at = pl.ds(pl.multiple_of(h * width, width), width)
        tops = top[:, :, at].astype(jnp.float32)
        top_k = tops[:, :per].reshape(top_rows, width).astype(jnp.bfloat16)
        top_v = tops[:, per:].reshape(top_rows, width).astype(jnp.bfloat16)
        side = full - edge

        def listed(slots, value):
            fine = tokens if value else 0
            pool = pool_rows if value else 0
            parts = []
            for k in slots:
                parts += [
                    left[k, h, pl.ds(mid + fine - side, tokens)],
                    own[k, h, pl.ds(fine, tokens)],
                    own[k, h, pl.ds(mid + fine, tokens)],
                    right[k, h, pl.ds(fine, tokens)],
                    left[k, h, pl.ds(low + pool - side, pool_rows)],
                    own[k, h, pl.ds(low + pool, pool_rows)],
                    right[k, h, pl.ds(low + pool, pool_rows)],
                ]
            parts.append(top_v if value else top_k)
            return jnp.concatenate(parts, axis=0)

        for slots in ((MATE, MINE, BY_MATE), (MINE, MATE, BY_MINE)):
            which = slots[0]
            scores = lax.dot_general(
                own[which, h, pl.ds(full, 2 * tokens)],
                listed(slots, False),
                (((1,), (1,)), ((), ())),
                preferred_element_type=jnp.float32,
            )
            added = bias[which, 0:2, 0:listed_count]
            scores = (scores * score_scale).reshape(2, tokens, -1) + added[:, None, :]
            peak = jnp.max(scores, axis=-1, keepdims=True)
            exponent = jnp.exp2(scores - peak)
            total = jnp.sum(exponent, axis=-1, keepdims=True)
            weights = (exponent * (1.0 / total)).astype(jnp.bfloat16)
            result = jnp.dot(
                weights.reshape(2 * tokens, -1),
                listed(slots, True),
                preferred_element_type=jnp.float32,
            )
            result = result.reshape(2, tokens, width).astype(jnp.bfloat16)
            if which == MATE:
                back[h] = result
                back_copy(h).start()
            else:
                out[0, 0, :, :, lanes(odd, h)] = result

    def step(t, _):
        @pl.when(t < heads)
        def _():
            give_copy(t).wait_recv()

            @pl.when(has_by_mate)
            def _():
                by_mine_copy(t).start()

            sideways(MATE, t)

        @pl.when(t + AHEAD < heads)
        def _():
            send_own(t + AHEAD)

        @pl.when(t + LOADS < heads)
        def _():
            load(t + LOADS)

        @pl.when(t >= ATTEND_LAG)
        def _():
            h = t - ATTEND_LAG

            @pl.when(h == 0)
            def _():
                bias_copy.wait_recv()
                for s in range(1, cols):
                    top_copy(s).wait_recv()

            for k, there in (
                (MINE, None),
                (MATE, None),
                (BY_MATE, has_by_mate),
                (BY_MINE, has_by_mine),
            ):
                @pl.when(has_left if there is None else there & has_left)
                def _():
                    to_right(k, h).wait_recv()

                @pl.when(has_right if there is None else there & has_right)
                def _():
                    to_left(k, h).wait_recv()

            attend(h)

        @pl.when((t >= FAR_LAG) & (t < heads + FAR_LAG))
        def _():
            h = t - FAR_LAG

            @pl.when(has_by_mate)
            def _():
                by_mate_copy(h).wait_recv()
                sideways(BY_MATE, h)

            @pl.when(has_by_mine)
            def _():
                by_mine_copy(h).wait_recv()
                sideways(BY_MINE, h)

        return 0

    lax.fori_loop(0, heads + ATTEND_LAG, step, 0)

    remote(give, own.at[MATE], give_send, mate_recv.at[0], mate, c).wait_send()
    bias_copy.wait_send()

    @pl.when(has_by_mate)
    def _():
        tiles = own.at[MATE, :, pl.ds(0, full)]
        remote(tiles, tiles, by_mine_send, by_mine_recv.at[0], mate_to, c).wait_send()

    @pl.when(has_by_mine)
    def _():
        tiles = own.at[MINE, :, pl.ds(0, full)]
        remote(tiles, tiles, by_mate_send, by_mate_recv.at[0], mine_to, c).wait_send()

    for k, there in ((MINE, None), (MATE, None), (BY_MATE, has_by_mate), (BY_MINE, has_by_mine)):
        @pl.when(has_left if there is None else there & has_left)
        def _():
            remote(
                right.at[k], right.at[k], left_send.at[k], right_recv.at[k, 0], r, c - 1
            ).wait_send()

        @pl.when(has_right if there is None else there & has_right)
        def _():
            remote(
                left.at[k], left.at[k], right_send.at[k], left_recv.at[k, 0], r, c + 1
            ).wait_send()

    for s in range(1, cols):
        top_copy(s).wait_send()
    returned = remote(back, back, back_send, back_recv, mate, c)
    returned.wait_send()
    returned.wait_recv()


def solution(mesh):
    row_count, col_count = mesh.shape["row"], mesh.shape["col"]

    def body(queries, keys, values, pool_keys, pool_values, top_keys, top_values, coarse_ids):
        tokens, model_width = queries.shape[3:]
        pool_blocks, pool_tokens, _ = pool_keys.shape
        pool_rows = pool_blocks * pool_tokens
        width = model_width // HEADS
        heads = HEADS // 2
        full = 4 * tokens + 2 * pool_rows
        edge = 2 * tokens + 2 * pool_rows
        whole = full + 2 * tokens
        per = top_keys.shape[1]
        listed = 3 * (4 * tokens + 3 * pool_rows) + col_count * per
        lanes = -(-listed // 128) * 128
        dims = (row_count, col_count, tokens, pool_rows, pool_blocks, heads, width, listed)
        dma = pltpu.SemaphoreType.DMA
        return pl.pallas_call(
            functools.partial(kernel, dims),
            out_shape=pltpu.VMEM(queries.shape, queries.dtype),
            in_specs=[pl.BlockSpec(memory_space=pltpu.HBM)] * 8,
            out_specs=pl.BlockSpec(memory_space=pltpu.VMEM),
            scratch_shapes=[
                pltpu.VMEM((4, heads, whole, width), jnp.bfloat16),
                pltpu.VMEM((heads, whole, width), jnp.bfloat16),
                pltpu.VMEM((4, heads, edge, width), jnp.bfloat16),
                pltpu.VMEM((4, heads, edge, width), jnp.bfloat16),
                pltpu.VMEM((heads, 2, tokens, width), jnp.bfloat16),
                pltpu.VMEM((col_count, 2 * per, model_width // 2), jnp.bfloat16),
                pltpu.VMEM((2, per, model_width // 2), jnp.bfloat16),
                pltpu.SMEM(coarse_ids.shape, jnp.int32),
                pltpu.VMEM((2, 8, lanes), jnp.float32),
                dma((heads,)),
                dma((heads,)),
                dma((2,)),
                dma,
                dma,
                dma((heads,)),
                dma,
                dma((heads,)),
                dma,
                dma((heads,)),
                dma((4,)),
                dma((4, heads)),
                dma((4,)),
                dma((4, heads)),
                dma((col_count,)),
                dma((col_count,)),
                dma,
                dma,
                dma,
                dma,
            ],
            compiler_params=pltpu.CompilerParams(
                collective_id=0, has_side_effects=True, vmem_limit_bytes=62 * 2**20
            ),
            cost_estimate=pl.CostEstimate(
                flops=4 * 2 * tokens * listed * model_width,
                bytes_accessed=8 * 2**20,
                transcendentals=2 * tokens * listed * HEADS,
            ),
        )(
            queries.reshape(2 * tokens, model_width),
            keys.reshape(2 * tokens, model_width),
            values.reshape(2 * tokens, model_width),
            pool_keys.reshape(pool_rows, model_width),
            pool_values.reshape(pool_rows, model_width),
            top_keys,
            top_values,
            coarse_ids,
        )

    placed = (
        P(None, "row", "col", None, None),
        P(None, "row", "col", None, None),
        P(None, "row", "col", None, None),
        P(("row", "col"), None, None),
        P(("row", "col"), None, None),
        P(None, "col", None),
        P(None, "col", None),
        P(None, "row", "col", None),
    )
    return jax.shard_map(
        body,
        mesh=mesh,
        in_specs=placed,
        out_specs=P(None, "row", "col", None, None),
        check_vma=False,
    )
```

```python
import functools
import math

import jax
import jax.numpy as jnp
from jax import lax
from jax.experimental import pallas as pl
from jax.experimental.pallas import tpu as pltpu
from jax.sharding import PartitionSpec as P

HEADS = 16
NEG_FILL = -1e30
HEADS_PER_CHUNK = 2
AHEAD = 3
FAR_LAG = 1
ATTEND_LAG = 3
PAIR = 2
NEAR, FAR = 0, 1


def kernel(
    dims,
    q_in,
    k_in,
    v_in,
    pk_in,
    pv_in,
    tk_in,
    tv_in,
    ids_in,
    out,
    mine,
    mine_left,
    mine_right,
    own,
    left,
    right,
    q_buf,
    top,
    top_own,
    ids,
    bias,
    load_sem,
    top_sem,
    ids_sem,
    q_sem,
    near_send,
    near_recv,
    far_send,
    far_recv,
    left_send,
    left_recv,
    right_send,
    right_recv,
    mine_send,
    mine_recv,
    top_send,
    top_recv,
):
    rows, cols, tokens, pool_rows, pool_blocks, chunks, width, head_width = dims
    pool_tokens = pool_rows // pool_blocks
    r = lax.axis_index("row")
    c = lax.axis_index("col")
    odd = lax.rem(r, 2)
    near_row = r + 1 - 2 * odd
    far_row = r - 1 + 2 * odd
    far_to = r + 2 - 4 * odd
    has_far = (far_row >= 0) & (far_row < rows)
    has_to = (far_to >= 0) & (far_to < rows)
    has_left = c > 0
    has_right = c < cols - 1
    low = 2 * tokens
    mid = low + 2 * pool_rows
    full = mid + 2 * tokens
    edge = mid

    def lanes(g):
        return pl.ds(pl.multiple_of(g * width, width), width)

    pieces = (
        (k_in.at[0, 0, 0], 0, tokens),
        (v_in.at[0, 0, 0], tokens, tokens),
        (pk_in, low, pool_rows),
        (pv_in, low + pool_rows, pool_rows),
        (k_in.at[0, 0, 1], mid, tokens),
        (v_in.at[0, 0, 1], mid + tokens, tokens),
    )
    for source, start, size in pieces:
        pltpu.make_async_copy(source, mine.at[pl.ds(start, size)], load_sem).start()

    barrier = pltpu.get_barrier_semaphore()

    def greet(there, row, col):
        @pl.when(there)
        def _():
            pl.semaphore_signal(
                barrier, inc=1, device_id=(row, col), device_id_type=pl.DeviceIdType.MESH
            )

    pl.semaphore_signal(
        barrier, inc=1, device_id=(near_row, c), device_id_type=pl.DeviceIdType.MESH
    )
    greet(r + 2 < rows, r + 2, c)
    greet(r >= 2, r - 2, c)
    for step in range(1, cols):
        pl.semaphore_signal(
            barrier,
            inc=1,
            device_id=(r, lax.rem(c + step, cols)),
            device_id_type=pl.DeviceIdType.MESH,
        )

    ids_copy = pltpu.make_async_copy(ids_in, ids, ids_sem)
    ids_copy.start()
    tk_copy = pltpu.make_async_copy(tk_in.at[0], top_own.at[0], top_sem.at[0])
    tk_copy.start()
    tv_copy = pltpu.make_async_copy(tv_in.at[0], top_own.at[1], top_sem.at[1])
    tv_copy.start()
    q_copy = pltpu.make_async_copy(q_in.at[0, 0], q_buf, q_sem)
    q_copy.start()

    greeted = (
        1
        + (r + 2 < rows).astype(jnp.int32)
        + (r >= 2).astype(jnp.int32)
        + (cols - 1)
    )
    pl.semaphore_wait(barrier, greeted)

    def remote(source, target, send, recv, row, col):
        return pltpu.make_async_remote_copy(
            src_ref=source,
            dst_ref=target,
            send_sem=send,
            recv_sem=recv,
            device_id=(row, col),
            device_id_type=pl.DeviceIdType.MESH,
        )

    def near_copy(g):
        return remote(
            mine.at[:, lanes(g)], own.at[NEAR, g], near_send, near_recv.at[g], near_row, c
        )

    def far_copy(g):
        return remote(own.at[NEAR, g], own.at[FAR, g], far_send, far_recv.at[g], far_to, c)

    def to_left(k, g, n):
        return remote(
            own.at[k, pl.ds(g, n), pl.ds(0, edge)],
            right.at[k, pl.ds(g, n)],
            left_send.at[k],
            right_recv.at[k, g],
            r,
            c - 1,
        )

    def to_right(k, g, n):
        return remote(
            own.at[k, pl.ds(g, n), pl.ds(full - edge, edge)],
            left.at[k, pl.ds(g, n)],
            right_send.at[k],
            left_recv.at[k, g],
            r,
            c + 1,
        )

    def sideways(k, g, n):
        @pl.when(has_left)
        def _():
            to_left(k, g, n).start()

        @pl.when(has_right)
        def _():
            to_right(k, g, n).start()

    mine_to_left = remote(
        mine.at[pl.ds(0, edge)], mine_right, mine_send.at[0], mine_recv.at[1], r, c - 1
    )
    mine_to_right = remote(
        mine.at[pl.ds(full - edge, edge)], mine_left, mine_send.at[1], mine_recv.at[0], r, c + 1
    )

    def top_copy(step):
        to = lax.rem(c + step, cols)
        return remote(top.at[c], top.at[c], top_send.at[step], top_recv.at[step], r, to)

    pltpu.make_async_copy(mine, mine, load_sem).wait()
    for g in range(min(AHEAD, chunks)):
        near_copy(g).start()

    @pl.when(has_left)
    def _():
        mine_to_left.start()

    @pl.when(has_right)
    def _():
        mine_to_right.start()

    tk_copy.wait()
    tv_copy.wait()
    ids_copy.wait()
    top[c] = jnp.concatenate(
        [top_own[0].astype(jnp.float32), top_own[1].astype(jnp.float32)], axis=0
    ).astype(jnp.bfloat16)

    for step in range(1, cols):
        top_copy(step).start()

    @pl.when(jnp.logical_not(has_far))
    def _():
        own[FAR] = jnp.zeros(own.shape[1:], own.dtype)

    @pl.when(jnp.logical_not(has_far & has_left))
    def _():
        left[FAR] = jnp.zeros(left.shape[1:], left.dtype)

    @pl.when(jnp.logical_not(has_far & has_right))
    def _():
        right[FAR] = jnp.zeros(right.shape[1:], right.dtype)

    @pl.when(jnp.logical_not(has_left))
    def _():
        left[NEAR] = jnp.zeros(left.shape[1:], left.dtype)
        mine_left[...] = jnp.zeros(mine_left.shape, mine_left.dtype)

    @pl.when(jnp.logical_not(has_right))
    def _():
        right[NEAR] = jnp.zeros(right.shape[1:], right.dtype)
        mine_right[...] = jnp.zeros(mine_right.shape, mine_right.dtype)

    top_rows = cols * tk_in.shape[1]
    for b in range(2):
        parts = []
        for row in (r, near_row, far_row):
            row_there = (row >= 0) & (row < rows)
            for slot in range(4):
                if slot in (b, b + 1, b + 2):
                    there = row_there
                    if slot == 0:
                        there = there & has_left
                    if slot == 3:
                        there = there & has_right
                    value = jnp.where(there, 0.0, NEG_FILL)
                else:
                    value = jnp.float32(NEG_FILL)
                parts.append(jnp.full((1, tokens), value, jnp.float32))
            for shift in (-1, 0, 1):
                there = row_there & (c + shift >= 0) & (c + shift < cols)
                base = (row * cols + c + shift) * pool_blocks
                for block in range(pool_blocks):
                    listed_here = jnp.int32(0)
                    for n in range(ids.shape[3]):
                        listed_here = listed_here | (ids[0, 0, b, n] == base + block).astype(
                            jnp.int32
                        )
                    listed_here = listed_here * there.astype(jnp.int32)
                    value = (1.0 - listed_here.astype(jnp.float32)) * NEG_FILL
                    parts.append(jnp.full((1, pool_tokens), value, jnp.float32))
        parts.append(jnp.zeros((1, top_rows), jnp.float32))
        at = 0
        for part in parts:
            bias[b : b + 1, at : at + part.shape[1]] = part
            at += part.shape[1]

    q_copy.wait()

    score_scale = math.log2(math.e) / math.sqrt(head_width)

    def attend(g):
        at = lanes(g)
        q_chunk = q_buf[:, :, at].reshape(2 * tokens, width)
        tops = top[:, :, at].astype(jnp.float32)
        per = tk_in.shape[1]
        top_k = tops[:, :per].reshape(top_rows, width).astype(jnp.bfloat16)
        top_v = tops[:, per:].reshape(top_rows, width).astype(jnp.bfloat16)

        def listed(head, value, top_part):
            lane = pl.ds(head * head_width, head_width)
            fine = tokens if value else 0
            pool = pool_rows if value else 0
            side = full - edge
            mine_lane = pl.ds(
                pl.multiple_of(g * width + head * head_width, head_width), head_width
            )
            parts = [
                mine_left[pl.ds(mid + fine - side, tokens), mine_lane],
                mine[pl.ds(fine, tokens), mine_lane],
                mine[pl.ds(mid + fine, tokens), mine_lane],
                mine_right[pl.ds(fine, tokens), mine_lane],
                mine_left[pl.ds(low + pool - side, pool_rows), mine_lane],
                mine[pl.ds(low + pool, pool_rows), mine_lane],
                mine_right[pl.ds(low + pool, pool_rows), mine_lane],
            ]
            for k in (NEAR, FAR):
                parts += [
                    left[k, g, pl.ds(mid + fine - side, tokens), lane],
                    own[k, g, pl.ds(fine, tokens), lane],
                    own[k, g, pl.ds(mid + fine, tokens), lane],
                    right[k, g, pl.ds(fine, tokens), lane],
                    left[k, g, pl.ds(low + pool - side, pool_rows), lane],
                    own[k, g, pl.ds(low + pool, pool_rows), lane],
                    right[k, g, pl.ds(low + pool, pool_rows), lane],
                ]
            parts.append(top_part[:, head * head_width : (head + 1) * head_width])
            return jnp.concatenate(parts, axis=0)

        for head in range(width // head_width):
            q_head = q_chunk[:, head * head_width : (head + 1) * head_width]
            scores = lax.dot_general(
                q_head,
                listed(head, False, top_k),
                (((1,), (1,)), ((), ())),
                preferred_element_type=jnp.float32,
            )
            scores = (scores * score_scale).reshape(2, tokens, -1) + bias[...][:, None, :]
            peak = jnp.max(scores, axis=-1, keepdims=True)
            exponent = jnp.exp2(scores - peak)
            total = jnp.sum(exponent, axis=-1, keepdims=True)
            weights = (exponent * (1.0 / total)).astype(jnp.bfloat16)
            result = jnp.dot(
                weights.reshape(2 * tokens, -1),
                listed(head, True, top_v),
                preferred_element_type=jnp.float32,
            )
            out_lane = pl.ds(
                pl.multiple_of(g * width + head * head_width, head_width), head_width
            )
            out[0, 0, :, :, out_lane] = result.reshape(2, tokens, head_width).astype(
                jnp.bfloat16
            )

    def step(t, _):
        @pl.when(t < chunks)
        def _():
            near_copy(t).wait_recv()

            @pl.when(has_to)
            def _():
                far_copy(t).start()

            @pl.when(lax.rem(t, PAIR) == PAIR - 1)
            def _():
                sideways(NEAR, t - (PAIR - 1), PAIR)

        @pl.when(t + AHEAD < chunks)
        def _():
            near_copy(t + AHEAD).start()

        @pl.when(t >= ATTEND_LAG)
        def _():
            g = t - ATTEND_LAG

            @pl.when(g == 0)
            def _():
                for s in range(1, cols):
                    top_copy(s).wait_recv()

            @pl.when((g == 0) & has_left)
            def _():
                mine_to_right.wait_recv()

            @pl.when((g == 0) & has_right)
            def _():
                mine_to_left.wait_recv()

            first = lax.rem(g, PAIR) == 0

            @pl.when(first & has_left)
            def _():
                to_right(NEAR, g, PAIR).wait_recv()

            @pl.when(first & has_right)
            def _():
                to_left(NEAR, g, PAIR).wait_recv()

            @pl.when(has_far & has_left)
            def _():
                to_right(FAR, g, 1).wait_recv()

            @pl.when(has_far & has_right)
            def _():
                to_left(FAR, g, 1).wait_recv()

            attend(g)

        @pl.when((t >= FAR_LAG) & (t < chunks + FAR_LAG) & has_far)
        def _():
            far_copy(t - FAR_LAG).wait_recv()
            sideways(FAR, t - FAR_LAG, 1)

        return 0

    lax.fori_loop(0, chunks + ATTEND_LAG, step, 0)

    remote(own.at[NEAR], own.at[NEAR], near_send, near_recv.at[0], near_row, c).wait_send()

    @pl.when(has_to)
    def _():
        remote(own.at[NEAR], own.at[FAR], far_send, far_recv.at[0], far_to, c).wait_send()

    def sent(k):
        @pl.when(has_left)
        def _():
            remote(
                own.at[k, :, pl.ds(0, edge)],
                right.at[k],
                left_send.at[k],
                right_recv.at[k, 0],
                r,
                c - 1,
            ).wait_send()

        @pl.when(has_right)
        def _():
            remote(
                own.at[k, :, pl.ds(full - edge, edge)],
                left.at[k],
                right_send.at[k],
                left_recv.at[k, 0],
                r,
                c + 1,
            ).wait_send()

    @pl.when(has_left)
    def _():
        mine_to_left.wait_send()

    @pl.when(has_right)
    def _():
        mine_to_right.wait_send()

    sent(NEAR)

    @pl.when(has_far)
    def _():
        sent(FAR)

    for s in range(1, cols):
        top_copy(s).wait_send()


def solution(mesh):
    row_count, col_count = mesh.shape["row"], mesh.shape["col"]

    def body(queries, keys, values, pool_keys, pool_values, top_keys, top_values, coarse_ids):
        tokens, model_width = queries.shape[3:]
        pool_blocks, pool_tokens, _ = pool_keys.shape
        pool_rows = pool_blocks * pool_tokens
        head_width = model_width // HEADS
        width = HEADS_PER_CHUNK * head_width
        chunks = model_width // width
        full = 4 * tokens + 2 * pool_rows
        edge = 2 * tokens + 2 * pool_rows
        per = top_keys.shape[1]
        listed = 3 * (4 * tokens + 3 * pool_rows) + col_count * per
        dims = (row_count, col_count, tokens, pool_rows, pool_blocks, chunks, width, head_width)
        dma = pltpu.SemaphoreType.DMA
        return pl.pallas_call(
            functools.partial(kernel, dims),
            out_shape=pltpu.VMEM(queries.shape, queries.dtype),
            in_specs=[pl.BlockSpec(memory_space=pltpu.HBM)] * 8,
            out_specs=pl.BlockSpec(memory_space=pltpu.VMEM),
            scratch_shapes=[
                pltpu.VMEM((full, model_width), jnp.bfloat16),
                pltpu.VMEM((edge, model_width), jnp.bfloat16),
                pltpu.VMEM((edge, model_width), jnp.bfloat16),
                pltpu.VMEM((2, chunks, full, width), jnp.bfloat16),
                pltpu.VMEM((2, chunks, edge, width), jnp.bfloat16),
                pltpu.VMEM((2, chunks, edge, width), jnp.bfloat16),
                pltpu.VMEM((2, tokens, model_width), jnp.bfloat16),
                pltpu.VMEM((col_count, 2 * per, model_width), jnp.bfloat16),
                pltpu.VMEM((2, per, model_width), jnp.bfloat16),
                pltpu.SMEM(coarse_ids.shape, jnp.int32),
                pltpu.VMEM((2, listed), jnp.float32),
                dma,
                dma((2,)),
                dma,
                dma,
                dma,
                dma((chunks,)),
                dma,
                dma((chunks,)),
                dma((2,)),
                dma((2, chunks)),
                dma((2,)),
                dma((2, chunks)),
                dma((2,)),
                dma((2,)),
                dma((col_count,)),
                dma((col_count,)),
            ],
            compiler_params=pltpu.CompilerParams(
                collective_id=0, has_side_effects=True, vmem_limit_bytes=62 * 2**20
            ),
            cost_estimate=pl.CostEstimate(
                flops=4 * 2 * tokens * listed * model_width,
                bytes_accessed=8 * 2**20,
                transcendentals=2 * tokens * listed * HEADS,
            ),
        )(
            queries,
            keys,
            values,
            pool_keys.reshape(pool_rows, model_width),
            pool_values.reshape(pool_rows, model_width),
            top_keys,
            top_values,
            coarse_ids,
        )

    placed = (
        P(None, "row", "col", None, None),
        P(None, "row", "col", None, None),
        P(None, "row", "col", None, None),
        P(("row", "col"), None, None),
        P(("row", "col"), None, None),
        P(None, "col", None),
        P(None, "col", None),
        P(None, "row", "col", None),
    )
    return jax.shard_map(
        body,
        mesh=mesh,
        in_specs=placed,
        out_specs=P(None, "row", "col", None, None),
        check_vma=False,
    )
```

```python
import functools
import math

import jax
import jax.numpy as jnp
from jax import lax
from jax.experimental import pallas as pl
from jax.experimental.pallas import tpu as pltpu
from jax.sharding import PartitionSpec as P

HEADS = 16
NEG_FILL = -1e30
HEADS_PER_CHUNK = 2
AHEAD = 3
FAR_LAG = 1
ATTEND_LAG = 3
PAIR = 2
NEAR, FAR = 0, 1


def kernel(
    dims,
    q_in,
    k_in,
    v_in,
    pk_in,
    pv_in,
    tk_in,
    tv_in,
    ids_in,
    out,
    mine,
    mine_left,
    mine_right,
    own,
    left,
    right,
    q_buf,
    top,
    top_own,
    ids,
    bias,
    side_bias,
    load_sem,
    top_sem,
    ids_sem,
    q_sem,
    near_send,
    near_recv,
    far_send,
    far_recv,
    left_send,
    left_recv,
    right_send,
    right_recv,
    mine_send,
    mine_recv,
    top_send,
    top_recv,
):
    rows, cols, tokens, pool_rows, pool_blocks, chunks, width, head_width = dims
    pool_tokens = pool_rows // pool_blocks
    r = lax.axis_index("row")
    c = lax.axis_index("col")
    odd = lax.rem(r, 2)
    near_row = r + 1 - 2 * odd
    far_row = r - 1 + 2 * odd
    far_to = r + 2 - 4 * odd
    has_far = (far_row >= 0) & (far_row < rows)
    has_to = (far_to >= 0) & (far_to < rows)
    has_left = c > 0
    has_right = c < cols - 1
    low = 2 * tokens
    mid = low + 2 * pool_rows
    full = mid + 2 * tokens
    edge = mid

    def lanes(g):
        return pl.ds(pl.multiple_of(g * width, width), width)

    pieces = (
        (k_in.at[0, 0, 0], 0, tokens),
        (v_in.at[0, 0, 0], tokens, tokens),
        (pk_in, low, pool_rows),
        (pv_in, low + pool_rows, pool_rows),
        (k_in.at[0, 0, 1], mid, tokens),
        (v_in.at[0, 0, 1], mid + tokens, tokens),
    )
    for source, start, size in pieces:
        pltpu.make_async_copy(source, mine.at[pl.ds(start, size)], load_sem).start()

    barrier = pltpu.get_barrier_semaphore()

    def greet(there, row, col):
        @pl.when(there)
        def _():
            pl.semaphore_signal(
                barrier, inc=1, device_id=(row, col), device_id_type=pl.DeviceIdType.MESH
            )

    pl.semaphore_signal(
        barrier, inc=1, device_id=(near_row, c), device_id_type=pl.DeviceIdType.MESH
    )
    greet(r + 2 < rows, r + 2, c)
    greet(r >= 2, r - 2, c)
    for step in range(1, cols):
        pl.semaphore_signal(
            barrier,
            inc=1,
            device_id=(r, lax.rem(c + step, cols)),
            device_id_type=pl.DeviceIdType.MESH,
        )

    ids_copy = pltpu.make_async_copy(ids_in, ids, ids_sem)
    ids_copy.start()
    tk_copy = pltpu.make_async_copy(tk_in.at[0], top_own.at[0], top_sem.at[0])
    tk_copy.start()
    tv_copy = pltpu.make_async_copy(tv_in.at[0], top_own.at[1], top_sem.at[1])
    tv_copy.start()
    q_copy = pltpu.make_async_copy(q_in.at[0, 0], q_buf, q_sem)
    q_copy.start()

    greeted = (
        1
        + (r + 2 < rows).astype(jnp.int32)
        + (r >= 2).astype(jnp.int32)
        + (cols - 1)
    )
    pl.semaphore_wait(barrier, greeted)

    def remote(source, target, send, recv, row, col):
        return pltpu.make_async_remote_copy(
            src_ref=source,
            dst_ref=target,
            send_sem=send,
            recv_sem=recv,
            device_id=(row, col),
            device_id_type=pl.DeviceIdType.MESH,
        )

    def near_copy(g):
        return remote(
            mine.at[:, lanes(g)], own.at[NEAR, g], near_send, near_recv.at[g], near_row, c
        )

    def far_copy(g):
        return remote(own.at[NEAR, g], own.at[FAR, g], far_send, far_recv.at[g], far_to, c)

    def to_left(k, g, n):
        return remote(
            own.at[k, pl.ds(g, n), pl.ds(0, edge)],
            right.at[k, pl.ds(g, n)],
            left_send.at[k],
            right_recv.at[k, g],
            r,
            c - 1,
        )

    def to_right(k, g, n):
        return remote(
            own.at[k, pl.ds(g, n), pl.ds(full - edge, edge)],
            left.at[k, pl.ds(g, n)],
            right_send.at[k],
            left_recv.at[k, g],
            r,
            c + 1,
        )

    def sideways(k, g, n):
        @pl.when(has_left)
        def _():
            to_left(k, g, n).start()

        @pl.when(has_right)
        def _():
            to_right(k, g, n).start()

    mine_to_left = remote(
        mine.at[pl.ds(0, edge)], mine_right, mine_send.at[0], mine_recv.at[1], r, c - 1
    )
    mine_to_right = remote(
        mine.at[pl.ds(full - edge, edge)], mine_left, mine_send.at[1], mine_recv.at[0], r, c + 1
    )

    def top_copy(step):
        to = lax.rem(c + step, cols)
        return remote(top.at[c], top.at[c], top_send.at[step], top_recv.at[step], r, to)

    pltpu.make_async_copy(mine, mine, load_sem).wait()
    for g in range(min(AHEAD, chunks)):
        near_copy(g).start()

    @pl.when(has_left)
    def _():
        mine_to_left.start()

    @pl.when(has_right)
    def _():
        mine_to_right.start()

    tk_copy.wait()
    tv_copy.wait()
    ids_copy.wait()
    top[c] = jnp.concatenate(
        [top_own[0].astype(jnp.float32), top_own[1].astype(jnp.float32)], axis=0
    ).astype(jnp.bfloat16)

    for step in range(1, cols):
        top_copy(step).start()

    @pl.when(jnp.logical_not(has_far))
    def _():
        own[FAR] = jnp.zeros(own.shape[1:], own.dtype)

    @pl.when(jnp.logical_not(has_far & has_left))
    def _():
        left[FAR] = jnp.zeros(left.shape[1:], left.dtype)

    @pl.when(jnp.logical_not(has_far & has_right))
    def _():
        right[FAR] = jnp.zeros(right.shape[1:], right.dtype)

    @pl.when(jnp.logical_not(has_left))
    def _():
        left[NEAR] = jnp.zeros(left.shape[1:], left.dtype)
        mine_left[...] = jnp.zeros(mine_left.shape, mine_left.dtype)

    @pl.when(jnp.logical_not(has_right))
    def _():
        right[NEAR] = jnp.zeros(right.shape[1:], right.dtype)
        mine_right[...] = jnp.zeros(mine_right.shape, mine_right.dtype)

    top_rows = cols * tk_in.shape[1]
    for b in range(2):
        beside = has_left if b == 0 else has_right
        far_beside = has_far & beside

        def fine(there, count):
            return jnp.full((1, count * tokens), jnp.where(there, 0.0, NEG_FILL), jnp.float32)

        shared = []
        for row, row_there, blocks in ((r, True, 1), (near_row, True, 2), (far_row, has_far, 2)):
            shared.append(fine(row_there, blocks))
            for shift in (-1, 0, 1):
                there = jnp.logical_and(row_there, (c + shift >= 0) & (c + shift < cols))
                base = (row * cols + c + shift) * pool_blocks
                for block in range(pool_blocks):
                    here = jnp.int32(0)
                    for n in range(ids.shape[3]):
                        here = here | (ids[0, 0, b, n] == base + block).astype(jnp.int32)
                    here = here * there.astype(jnp.int32)
                    value = (1.0 - here.astype(jnp.float32)) * NEG_FILL
                    shared.append(jnp.full((1, pool_tokens), value, jnp.float32))
        shared.append(jnp.zeros((1, top_rows), jnp.float32))
        private = [fine(beside, 2), fine(far_beside, 1), jnp.zeros((1, tokens), jnp.float32)]
        for target, parts in ((bias, shared), (side_bias, private)):
            at = 0
            for part in parts:
                target[b : b + 1, at : at + part.shape[1]] = part
                at += part.shape[1]

    q_copy.wait()

    score_scale = math.log2(math.e) / math.sqrt(head_width)

    def attend(g):
        at = lanes(g)
        q_chunk = q_buf[:, :, at].reshape(2 * tokens, width)
        tops = top[:, :, at].astype(jnp.float32)
        per = tk_in.shape[1]
        top_k = tops[:, :per].reshape(top_rows, width).astype(jnp.bfloat16)
        top_v = tops[:, per:].reshape(top_rows, width).astype(jnp.bfloat16)

        side = full - edge

        def pieces_of(head, value):
            lane = pl.ds(head * head_width, head_width)
            mine_lane = pl.ds(
                pl.multiple_of(g * width + head * head_width, head_width), head_width
            )
            fine = tokens if value else 0
            pool = pool_rows if value else 0
            top_part = top_v if value else top_k
            first = pl.ds(fine, tokens)
            second = pl.ds(mid + fine, tokens)
            left_block = pl.ds(mid + fine - side, tokens)
            left_pool = pl.ds(low + pool - side, pool_rows)
            pools = pl.ds(low + pool, pool_rows)
            mine_first = mine[first, mine_lane]
            shared = [
                mine[second, mine_lane],
                mine_left[left_pool, mine_lane],
                mine[pools, mine_lane],
                mine_right[pools, mine_lane],
            ]
            for k in (NEAR, FAR):
                shared += [
                    own[k, g, first, lane],
                    own[k, g, second, lane],
                    left[k, g, left_pool, lane],
                    own[k, g, pools, lane],
                    right[k, g, pools, lane],
                ]
            shared.append(top_part[:, head * head_width : (head + 1) * head_width])
            low_side = [
                mine_left[left_block, mine_lane],
                left[NEAR, g, left_block, lane],
                left[FAR, g, left_block, lane],
                mine_first,
            ]
            high_side = [
                mine_right[first, mine_lane],
                right[NEAR, g, first, lane],
                right[FAR, g, first, lane],
                mine_first,
            ]
            return [jnp.concatenate(part, axis=0) for part in (shared, low_side, high_side)]

        def product(x, y):
            return lax.dot_general(
                x, y, (((1,), (1,)), ((), ())), preferred_element_type=jnp.float32
            )

        def scores_of(head):
            q_head = q_chunk[:, head * head_width : (head + 1) * head_width]
            shared, low_side, high_side = pieces_of(head, False)
            both = product(q_head, shared).reshape(2, tokens, -1)
            alone = jnp.stack(
                [product(q_head[:tokens], low_side), product(q_head[tokens:], high_side)]
            )
            return (
                both * score_scale + bias[...][:, None, :],
                alone * score_scale + side_bias[...][:, None, :],
            )

        def weights_of(both, alone):
            peak = jnp.maximum(
                jnp.max(both, axis=-1, keepdims=True), jnp.max(alone, axis=-1, keepdims=True)
            )
            both = jnp.exp2(both - peak)
            alone = jnp.exp2(alone - peak)
            total = jnp.sum(both, axis=-1, keepdims=True) + jnp.sum(alone, axis=-1, keepdims=True)
            share = 1.0 / total
            return (both * share).astype(jnp.bfloat16), (alone * share).astype(jnp.bfloat16)

        def attended(head, both, alone):
            shared, low_side, high_side = pieces_of(head, True)
            result = jnp.dot(
                both.reshape(2 * tokens, -1), shared, preferred_element_type=jnp.float32
            ).reshape(2, tokens, head_width)
            result = result + jnp.stack(
                [
                    jnp.dot(alone[0], low_side, preferred_element_type=jnp.float32),
                    jnp.dot(alone[1], high_side, preferred_element_type=jnp.float32),
                ]
            )
            out_lane = pl.ds(
                pl.multiple_of(g * width + head * head_width, head_width), head_width
            )
            out[0, 0, :, :, out_lane] = result.astype(jnp.bfloat16)

        count = width // head_width
        scores = [scores_of(head) for head in range(count)]
        weights = [weights_of(*pair) for pair in scores]
        for head in range(count):
            attended(head, *weights[head])

    def step(t, _):
        @pl.when(t < chunks)
        def _():
            near_copy(t).wait_recv()

            @pl.when(has_to)
            def _():
                far_copy(t).start()

            @pl.when(lax.rem(t, PAIR) == PAIR - 1)
            def _():
                sideways(NEAR, t - (PAIR - 1), PAIR)

        @pl.when(t + AHEAD < chunks)
        def _():
            near_copy(t + AHEAD).start()

        @pl.when(t >= ATTEND_LAG)
        def _():
            g = t - ATTEND_LAG

            @pl.when(g == 0)
            def _():
                for s in range(1, cols):
                    top_copy(s).wait_recv()

            @pl.when((g == 0) & has_left)
            def _():
                mine_to_right.wait_recv()

            @pl.when((g == 0) & has_right)
            def _():
                mine_to_left.wait_recv()

            first = lax.rem(g, PAIR) == 0

            @pl.when(first & has_left)
            def _():
                to_right(NEAR, g, PAIR).wait_recv()

            @pl.when(first & has_right)
            def _():
                to_left(NEAR, g, PAIR).wait_recv()

            @pl.when(has_far & has_left)
            def _():
                to_right(FAR, g, 1).wait_recv()

            @pl.when(has_far & has_right)
            def _():
                to_left(FAR, g, 1).wait_recv()

            attend(g)

        @pl.when((t >= FAR_LAG) & (t < chunks + FAR_LAG) & has_far)
        def _():
            far_copy(t - FAR_LAG).wait_recv()
            sideways(FAR, t - FAR_LAG, 1)

        return 0

    lax.fori_loop(0, chunks + ATTEND_LAG, step, 0)

    remote(own.at[NEAR], own.at[NEAR], near_send, near_recv.at[0], near_row, c).wait_send()

    @pl.when(has_to)
    def _():
        remote(own.at[NEAR], own.at[FAR], far_send, far_recv.at[0], far_to, c).wait_send()

    def sent(k):
        @pl.when(has_left)
        def _():
            remote(
                own.at[k, :, pl.ds(0, edge)],
                right.at[k],
                left_send.at[k],
                right_recv.at[k, 0],
                r,
                c - 1,
            ).wait_send()

        @pl.when(has_right)
        def _():
            remote(
                own.at[k, :, pl.ds(full - edge, edge)],
                left.at[k],
                right_send.at[k],
                left_recv.at[k, 0],
                r,
                c + 1,
            ).wait_send()

    @pl.when(has_left)
    def _():
        mine_to_left.wait_send()

    @pl.when(has_right)
    def _():
        mine_to_right.wait_send()

    sent(NEAR)

    @pl.when(has_far)
    def _():
        sent(FAR)

    for s in range(1, cols):
        top_copy(s).wait_send()


def solution(mesh):
    row_count, col_count = mesh.shape["row"], mesh.shape["col"]

    def body(queries, keys, values, pool_keys, pool_values, top_keys, top_values, coarse_ids):
        tokens, model_width = queries.shape[3:]
        pool_blocks, pool_tokens, _ = pool_keys.shape
        pool_rows = pool_blocks * pool_tokens
        head_width = model_width // HEADS
        width = HEADS_PER_CHUNK * head_width
        chunks = model_width // width
        full = 4 * tokens + 2 * pool_rows
        edge = 2 * tokens + 2 * pool_rows
        per = top_keys.shape[1]
        listed = 5 * tokens + 9 * pool_rows + col_count * per
        dims = (row_count, col_count, tokens, pool_rows, pool_blocks, chunks, width, head_width)
        dma = pltpu.SemaphoreType.DMA
        return pl.pallas_call(
            functools.partial(kernel, dims),
            out_shape=pltpu.VMEM(queries.shape, queries.dtype),
            in_specs=[pl.BlockSpec(memory_space=pltpu.HBM)] * 8,
            out_specs=pl.BlockSpec(memory_space=pltpu.VMEM),
            scratch_shapes=[
                pltpu.VMEM((full, model_width), jnp.bfloat16),
                pltpu.VMEM((edge, model_width), jnp.bfloat16),
                pltpu.VMEM((edge, model_width), jnp.bfloat16),
                pltpu.VMEM((2, chunks, full, width), jnp.bfloat16),
                pltpu.VMEM((2, chunks, edge, width), jnp.bfloat16),
                pltpu.VMEM((2, chunks, edge, width), jnp.bfloat16),
                pltpu.VMEM((2, tokens, model_width), jnp.bfloat16),
                pltpu.VMEM((col_count, 2 * per, model_width), jnp.bfloat16),
                pltpu.VMEM((2, per, model_width), jnp.bfloat16),
                pltpu.SMEM(coarse_ids.shape, jnp.int32),
                pltpu.VMEM((2, listed), jnp.float32),
                pltpu.VMEM((2, 4 * tokens), jnp.float32),
                dma,
                dma((2,)),
                dma,
                dma,
                dma,
                dma((chunks,)),
                dma,
                dma((chunks,)),
                dma((2,)),
                dma((2, chunks)),
                dma((2,)),
                dma((2, chunks)),
                dma((2,)),
                dma((2,)),
                dma((col_count,)),
                dma((col_count,)),
            ],
            compiler_params=pltpu.CompilerParams(
                collective_id=0, has_side_effects=True, vmem_limit_bytes=62 * 2**20
            ),
            cost_estimate=pl.CostEstimate(
                flops=4 * 2 * tokens * (listed + 4 * tokens) * model_width,
                bytes_accessed=8 * 2**20,
                transcendentals=2 * tokens * (listed + 4 * tokens) * HEADS,
            ),
        )(
            queries,
            keys,
            values,
            pool_keys.reshape(pool_rows, model_width),
            pool_values.reshape(pool_rows, model_width),
            top_keys,
            top_values,
            coarse_ids,
        )

    placed = (
        P(None, "row", "col", None, None),
        P(None, "row", "col", None, None),
        P(None, "row", "col", None, None),
        P(("row", "col"), None, None),
        P(("row", "col"), None, None),
        P(None, "col", None),
        P(None, "col", None),
        P(None, "row", "col", None),
    )
    return jax.shard_map(
        body,
        mesh=mesh,
        in_specs=placed,
        out_specs=P(None, "row", "col", None, None),
        check_vma=False,
    )
```

```python
import functools
import math

import jax
import jax.numpy as jnp
from jax import lax
from jax.experimental import pallas as pl
from jax.experimental.pallas import tpu as pltpu
from jax.sharding import PartitionSpec as P

HEADS = 16
NEG_FILL = -1e30
HEADS_PER_CHUNK = 2
AHEAD = 3
FAR_LAG = 1
ATTEND_LAG = 3
PAIR = 2
NEAR, FAR = 0, 1


def kernel(
    dims,
    q_in,
    k_in,
    v_in,
    pk_in,
    pv_in,
    tk_in,
    tv_in,
    ids_in,
    out,
    mine,
    mine_left,
    mine_right,
    own,
    left,
    right,
    q_buf,
    top,
    top_own,
    ids,
    bias,
    side_bias,
    load_sem,
    top_sem,
    ids_sem,
    q_sem,
    near_send,
    near_recv,
    far_send,
    far_recv,
    left_send,
    left_recv,
    right_send,
    right_recv,
    mine_send,
    mine_recv,
    top_send,
    top_recv,
):
    rows, cols, tokens, pool_rows, pool_blocks, chunks, width, head_width = dims
    pool_tokens = pool_rows // pool_blocks
    r = lax.axis_index("row")
    c = lax.axis_index("col")
    odd = lax.rem(r, 2)
    near_row = r + 1 - 2 * odd
    far_row = r - 1 + 2 * odd
    far_to = r + 2 - 4 * odd
    has_far = (far_row >= 0) & (far_row < rows)
    has_to = (far_to >= 0) & (far_to < rows)
    has_left = c > 0
    has_right = c < cols - 1
    low = 2 * tokens
    mid = low + 2 * pool_rows
    full = mid + 2 * tokens
    edge = mid

    def lanes(g):
        return pl.ds(pl.multiple_of(g * width, width), width)

    pieces = (
        (k_in.at[0, 0, 0], 0, tokens),
        (v_in.at[0, 0, 0], tokens, tokens),
        (pk_in, low, pool_rows),
        (pv_in, low + pool_rows, pool_rows),
        (k_in.at[0, 0, 1], mid, tokens),
        (v_in.at[0, 0, 1], mid + tokens, tokens),
    )
    for source, start, size in pieces:
        pltpu.make_async_copy(source, mine.at[pl.ds(start, size)], load_sem).start()

    barrier = pltpu.get_barrier_semaphore()

    def greet(there, row, col):
        @pl.when(there)
        def _():
            pl.semaphore_signal(
                barrier, inc=1, device_id=(row, col), device_id_type=pl.DeviceIdType.MESH
            )

    pl.semaphore_signal(
        barrier, inc=1, device_id=(near_row, c), device_id_type=pl.DeviceIdType.MESH
    )
    greet(r + 2 < rows, r + 2, c)
    greet(r >= 2, r - 2, c)
    for step in range(1, cols):
        pl.semaphore_signal(
            barrier,
            inc=1,
            device_id=(r, lax.rem(c + step, cols)),
            device_id_type=pl.DeviceIdType.MESH,
        )

    ids_copy = pltpu.make_async_copy(ids_in, ids, ids_sem)
    ids_copy.start()
    tk_copy = pltpu.make_async_copy(tk_in.at[0], top_own.at[0], top_sem.at[0])
    tk_copy.start()
    tv_copy = pltpu.make_async_copy(tv_in.at[0], top_own.at[1], top_sem.at[1])
    tv_copy.start()
    q_copy = pltpu.make_async_copy(q_in.at[0, 0], q_buf, q_sem)
    q_copy.start()

    greeted = (
        1
        + (r + 2 < rows).astype(jnp.int32)
        + (r >= 2).astype(jnp.int32)
        + (cols - 1)
    )
    pl.semaphore_wait(barrier, greeted)

    def remote(source, target, send, recv, row, col):
        return pltpu.make_async_remote_copy(
            src_ref=source,
            dst_ref=target,
            send_sem=send,
            recv_sem=recv,
            device_id=(row, col),
            device_id_type=pl.DeviceIdType.MESH,
        )

    def near_copy(g):
        return remote(
            mine.at[:, lanes(g)], own.at[NEAR, g], near_send, near_recv.at[g], near_row, c
        )

    def far_copy(g):
        return remote(own.at[NEAR, g], own.at[FAR, g], far_send, far_recv.at[g], far_to, c)

    def to_left(k, g, n):
        return remote(
            own.at[k, pl.ds(g, n), pl.ds(0, edge)],
            right.at[k, pl.ds(g, n)],
            left_send.at[k],
            right_recv.at[k, g],
            r,
            c - 1,
        )

    def to_right(k, g, n):
        return remote(
            own.at[k, pl.ds(g, n), pl.ds(full - edge, edge)],
            left.at[k, pl.ds(g, n)],
            right_send.at[k],
            left_recv.at[k, g],
            r,
            c + 1,
        )

    def sideways(k, g, n):
        @pl.when(has_left)
        def _():
            to_left(k, g, n).start()

        @pl.when(has_right)
        def _():
            to_right(k, g, n).start()

    def piece(p):
        return pl.ds(pl.multiple_of(p * PAIR * width, PAIR * width), PAIR * width)

    def mine_to_left(p):
        return remote(
            mine.at[pl.ds(0, edge), piece(p)],
            mine_right.at[:, piece(p)],
            mine_send.at[0],
            mine_recv.at[1, p],
            r,
            c - 1,
        )

    def mine_to_right(p):
        return remote(
            mine.at[pl.ds(full - edge, edge), piece(p)],
            mine_left.at[:, piece(p)],
            mine_send.at[1],
            mine_recv.at[0, p],
            r,
            c + 1,
        )

    def mine_sideways(p):
        @pl.when(has_left)
        def _():
            mine_to_left(p).start()

        @pl.when(has_right)
        def _():
            mine_to_right(p).start()

    def top_copy(step):
        to = lax.rem(c + step, cols)
        return remote(top.at[c], top.at[c], top_send.at[step], top_recv.at[step], r, to)

    pltpu.make_async_copy(mine, mine, load_sem).wait()
    for g in range(min(AHEAD, chunks)):
        near_copy(g).start()

    mine_sideways(0)
    tk_copy.wait()
    tv_copy.wait()
    ids_copy.wait()
    top[c] = jnp.concatenate(
        [top_own[0].astype(jnp.float32), top_own[1].astype(jnp.float32)], axis=0
    ).astype(jnp.bfloat16)

    for step in range(1, cols):
        top_copy(step).start()

    @pl.when(jnp.logical_not(has_far))
    def _():
        own[FAR] = jnp.zeros(own.shape[1:], own.dtype)

    @pl.when(jnp.logical_not(has_far & has_left))
    def _():
        left[FAR] = jnp.zeros(left.shape[1:], left.dtype)

    @pl.when(jnp.logical_not(has_far & has_right))
    def _():
        right[FAR] = jnp.zeros(right.shape[1:], right.dtype)

    @pl.when(jnp.logical_not(has_left))
    def _():
        left[NEAR] = jnp.zeros(left.shape[1:], left.dtype)
        mine_left[...] = jnp.zeros(mine_left.shape, mine_left.dtype)

    @pl.when(jnp.logical_not(has_right))
    def _():
        right[NEAR] = jnp.zeros(right.shape[1:], right.dtype)
        mine_right[...] = jnp.zeros(mine_right.shape, mine_right.dtype)

    top_rows = cols * tk_in.shape[1]
    for b in range(2):
        beside = has_left if b == 0 else has_right
        far_beside = has_far & beside

        def fine(there, count):
            return jnp.full((1, count * tokens), jnp.where(there, 0.0, NEG_FILL), jnp.float32)

        shared = []
        for row, row_there, blocks in ((r, True, 1), (near_row, True, 2), (far_row, has_far, 2)):
            shared.append(fine(row_there, blocks))
            for shift in (-1, 0, 1):
                there = jnp.logical_and(row_there, (c + shift >= 0) & (c + shift < cols))
                base = (row * cols + c + shift) * pool_blocks
                for block in range(pool_blocks):
                    here = jnp.int32(0)
                    for n in range(ids.shape[3]):
                        here = here | (ids[0, 0, b, n] == base + block).astype(jnp.int32)
                    here = here * there.astype(jnp.int32)
                    value = (1.0 - here.astype(jnp.float32)) * NEG_FILL
                    shared.append(jnp.full((1, pool_tokens), value, jnp.float32))
        shared.append(jnp.zeros((1, top_rows), jnp.float32))
        private = [fine(beside, 2), fine(far_beside, 1), jnp.zeros((1, tokens), jnp.float32)]
        for target, parts in ((bias, shared), (side_bias, private)):
            at = 0
            for part in parts:
                target[b : b + 1, at : at + part.shape[1]] = part
                at += part.shape[1]

    q_copy.wait()

    score_scale = math.log2(math.e) / math.sqrt(head_width)

    def attend(g):
        at = lanes(g)
        q_chunk = q_buf[:, :, at].reshape(2 * tokens, width)
        tops = top[:, :, at].astype(jnp.float32)
        per = tk_in.shape[1]
        top_k = tops[:, :per].reshape(top_rows, width).astype(jnp.bfloat16)
        top_v = tops[:, per:].reshape(top_rows, width).astype(jnp.bfloat16)

        side = full - edge

        def pieces_of(head, value):
            lane = pl.ds(head * head_width, head_width)
            mine_lane = pl.ds(
                pl.multiple_of(g * width + head * head_width, head_width), head_width
            )
            fine = tokens if value else 0
            pool = pool_rows if value else 0
            top_part = top_v if value else top_k
            first = pl.ds(fine, tokens)
            second = pl.ds(mid + fine, tokens)
            left_block = pl.ds(mid + fine - side, tokens)
            left_pool = pl.ds(low + pool - side, pool_rows)
            pools = pl.ds(low + pool, pool_rows)
            mine_first = mine[first, mine_lane]
            shared = [
                mine[second, mine_lane],
                mine_left[left_pool, mine_lane],
                mine[pools, mine_lane],
                mine_right[pools, mine_lane],
            ]
            for k in (NEAR, FAR):
                shared += [
                    own[k, g, first, lane],
                    own[k, g, second, lane],
                    left[k, g, left_pool, lane],
                    own[k, g, pools, lane],
                    right[k, g, pools, lane],
                ]
            shared.append(top_part[:, head * head_width : (head + 1) * head_width])
            low_side = [
                mine_left[left_block, mine_lane],
                left[NEAR, g, left_block, lane],
                left[FAR, g, left_block, lane],
                mine_first,
            ]
            high_side = [
                mine_right[first, mine_lane],
                right[NEAR, g, first, lane],
                right[FAR, g, first, lane],
                mine_first,
            ]
            return [jnp.concatenate(part, axis=0) for part in (shared, low_side, high_side)]

        def product(x, y):
            return lax.dot_general(
                x, y, (((1,), (1,)), ((), ())), preferred_element_type=jnp.float32
            )

        def scores_of(head):
            q_head = q_chunk[:, head * head_width : (head + 1) * head_width]
            shared, low_side, high_side = pieces_of(head, False)
            both = product(q_head, shared).reshape(2, tokens, -1)
            alone = jnp.stack(
                [product(q_head[:tokens], low_side), product(q_head[tokens:], high_side)]
            )
            return (
                both * score_scale + bias[...][:, None, :],
                alone * score_scale + side_bias[...][:, None, :],
            )

        def weights_of(both, alone):
            peak = jnp.maximum(
                jnp.max(both, axis=-1, keepdims=True), jnp.max(alone, axis=-1, keepdims=True)
            )
            both = jnp.exp2(both - peak)
            alone = jnp.exp2(alone - peak)
            total = jnp.sum(both, axis=-1, keepdims=True) + jnp.sum(alone, axis=-1, keepdims=True)
            share = 1.0 / total
            return (both * share).astype(jnp.bfloat16), (alone * share).astype(jnp.bfloat16)

        def attended(head, both, alone):
            shared, low_side, high_side = pieces_of(head, True)
            result = jnp.dot(
                both.reshape(2 * tokens, -1), shared, preferred_element_type=jnp.float32
            ).reshape(2, tokens, head_width)
            result = result + jnp.stack(
                [
                    jnp.dot(alone[0], low_side, preferred_element_type=jnp.float32),
                    jnp.dot(alone[1], high_side, preferred_element_type=jnp.float32),
                ]
            )
            out_lane = pl.ds(
                pl.multiple_of(g * width + head * head_width, head_width), head_width
            )
            out[0, 0, :, :, out_lane] = result.astype(jnp.bfloat16)

        count = width // head_width
        scores = [scores_of(head) for head in range(count)]
        weights = [weights_of(*pair) for pair in scores]
        for head in range(count):
            attended(head, *weights[head])

    def step(t, _):
        @pl.when(t < chunks)
        def _():
            near_copy(t).wait_recv()

            @pl.when(has_to)
            def _():
                far_copy(t).start()

            @pl.when(lax.rem(t, PAIR) == PAIR - 1)
            def _():
                sideways(NEAR, t - (PAIR - 1), PAIR)

            @pl.when((lax.rem(t, PAIR) == PAIR - 1) & (t + 1 < chunks))
            def _():
                mine_sideways((t + 1) // PAIR)

        @pl.when(t + AHEAD < chunks)
        def _():
            near_copy(t + AHEAD).start()

        @pl.when(t >= ATTEND_LAG)
        def _():
            g = t - ATTEND_LAG

            @pl.when(g == 0)
            def _():
                for s in range(1, cols):
                    top_copy(s).wait_recv()

            first = lax.rem(g, PAIR) == 0

            @pl.when(first & has_left)
            def _():
                mine_to_right(g // PAIR).wait_recv()
                to_right(NEAR, g, PAIR).wait_recv()

            @pl.when(first & has_right)
            def _():
                mine_to_left(g // PAIR).wait_recv()
                to_left(NEAR, g, PAIR).wait_recv()

            @pl.when(has_far & has_left)
            def _():
                to_right(FAR, g, 1).wait_recv()

            @pl.when(has_far & has_right)
            def _():
                to_left(FAR, g, 1).wait_recv()

            attend(g)

        @pl.when((t >= FAR_LAG) & (t < chunks + FAR_LAG) & has_far)
        def _():
            far_copy(t - FAR_LAG).wait_recv()
            sideways(FAR, t - FAR_LAG, 1)

        return 0

    lax.fori_loop(0, chunks + ATTEND_LAG, step, 0)

    remote(own.at[NEAR], own.at[NEAR], near_send, near_recv.at[0], near_row, c).wait_send()

    @pl.when(has_to)
    def _():
        remote(own.at[NEAR], own.at[FAR], far_send, far_recv.at[0], far_to, c).wait_send()

    def sent(k):
        @pl.when(has_left)
        def _():
            remote(
                own.at[k, :, pl.ds(0, edge)],
                right.at[k],
                left_send.at[k],
                right_recv.at[k, 0],
                r,
                c - 1,
            ).wait_send()

        @pl.when(has_right)
        def _():
            remote(
                own.at[k, :, pl.ds(full - edge, edge)],
                left.at[k],
                right_send.at[k],
                left_recv.at[k, 0],
                r,
                c + 1,
            ).wait_send()

    @pl.when(has_left)
    def _():
        remote(
            mine_right, mine_right, mine_send.at[0], mine_recv.at[1, 0], r, c - 1
        ).wait_send()

    @pl.when(has_right)
    def _():
        remote(
            mine_left, mine_left, mine_send.at[1], mine_recv.at[0, 0], r, c + 1
        ).wait_send()

    sent(NEAR)

    @pl.when(has_far)
    def _():
        sent(FAR)

    for s in range(1, cols):
        top_copy(s).wait_send()


def solution(mesh):
    row_count, col_count = mesh.shape["row"], mesh.shape["col"]

    def body(queries, keys, values, pool_keys, pool_values, top_keys, top_values, coarse_ids):
        tokens, model_width = queries.shape[3:]
        pool_blocks, pool_tokens, _ = pool_keys.shape
        pool_rows = pool_blocks * pool_tokens
        head_width = model_width // HEADS
        width = HEADS_PER_CHUNK * head_width
        chunks = model_width // width
        full = 4 * tokens + 2 * pool_rows
        edge = 2 * tokens + 2 * pool_rows
        per = top_keys.shape[1]
        listed = 5 * tokens + 9 * pool_rows + col_count * per
        dims = (row_count, col_count, tokens, pool_rows, pool_blocks, chunks, width, head_width)
        dma = pltpu.SemaphoreType.DMA
        return pl.pallas_call(
            functools.partial(kernel, dims),
            out_shape=pltpu.VMEM(queries.shape, queries.dtype),
            in_specs=[pl.BlockSpec(memory_space=pltpu.HBM)] * 8,
            out_specs=pl.BlockSpec(memory_space=pltpu.VMEM),
            scratch_shapes=[
                pltpu.VMEM((full, model_width), jnp.bfloat16),
                pltpu.VMEM((edge, model_width), jnp.bfloat16),
                pltpu.VMEM((edge, model_width), jnp.bfloat16),
                pltpu.VMEM((2, chunks, full, width), jnp.bfloat16),
                pltpu.VMEM((2, chunks, edge, width), jnp.bfloat16),
                pltpu.VMEM((2, chunks, edge, width), jnp.bfloat16),
                pltpu.VMEM((2, tokens, model_width), jnp.bfloat16),
                pltpu.VMEM((col_count, 2 * per, model_width), jnp.bfloat16),
                pltpu.VMEM((2, per, model_width), jnp.bfloat16),
                pltpu.SMEM(coarse_ids.shape, jnp.int32),
                pltpu.VMEM((2, listed), jnp.float32),
                pltpu.VMEM((2, 4 * tokens), jnp.float32),
                dma,
                dma((2,)),
                dma,
                dma,
                dma,
                dma((chunks,)),
                dma,
                dma((chunks,)),
                dma((2,)),
                dma((2, chunks)),
                dma((2,)),
                dma((2, chunks)),
                dma((2,)),
                dma((2, chunks // PAIR)),
                dma((col_count,)),
                dma((col_count,)),
            ],
            compiler_params=pltpu.CompilerParams(
                collective_id=0, has_side_effects=True, vmem_limit_bytes=62 * 2**20
            ),
            cost_estimate=pl.CostEstimate(
                flops=4 * 2 * tokens * (listed + 4 * tokens) * model_width,
                bytes_accessed=8 * 2**20,
                transcendentals=2 * tokens * (listed + 4 * tokens) * HEADS,
            ),
        )(
            queries,
            keys,
            values,
            pool_keys.reshape(pool_rows, model_width),
            pool_values.reshape(pool_rows, model_width),
            top_keys,
            top_values,
            coarse_ids,
        )

    placed = (
        P(None, "row", "col", None, None),
        P(None, "row", "col", None, None),
        P(None, "row", "col", None, None),
        P(("row", "col"), None, None),
        P(("row", "col"), None, None),
        P(None, "col", None),
        P(None, "col", None),
        P(None, "row", "col", None),
    )
    return jax.shard_map(
        body,
        mesh=mesh,
        in_specs=placed,
        out_specs=P(None, "row", "col", None, None),
        check_vma=False,
    )
```

```python
import functools
import math

import jax
import jax.numpy as jnp
from jax import lax
from jax.experimental import pallas as pl
from jax.experimental.pallas import tpu as pltpu
from jax.sharding import PartitionSpec as P

HEADS = 16
NEG_FILL = -1e30
HEADS_PER_CHUNK = 1
AHEAD = 5
FAR_LAG = 2
ATTEND_LAG = 3
PAIR = 2
NEAR, FAR = 0, 1


def kernel(
    dims,
    q_in,
    k_in,
    v_in,
    pk_in,
    pv_in,
    tk_in,
    tv_in,
    ids_in,
    out,
    mine,
    mine_left,
    mine_right,
    own,
    left,
    right,
    q_buf,
    top,
    top_own,
    ids,
    bias,
    side_bias,
    load_sem,
    top_sem,
    ids_sem,
    q_sem,
    near_send,
    near_recv,
    far_send,
    far_recv,
    left_send,
    left_recv,
    right_send,
    right_recv,
    mine_send,
    mine_recv,
    top_send,
    top_recv,
):
    rows, cols, tokens, pool_rows, pool_blocks, chunks, width, head_width = dims
    pool_tokens = pool_rows // pool_blocks
    r = lax.axis_index("row")
    c = lax.axis_index("col")
    odd = lax.rem(r, 2)
    near_row = r + 1 - 2 * odd
    far_row = r - 1 + 2 * odd
    far_to = r + 2 - 4 * odd
    has_far = (far_row >= 0) & (far_row < rows)
    has_to = (far_to >= 0) & (far_to < rows)
    has_left = c > 0
    has_right = c < cols - 1
    low = 2 * tokens
    mid = low + 2 * pool_rows
    full = mid + 2 * tokens
    edge = mid

    def lanes(g):
        return pl.ds(pl.multiple_of(g * width, width), width)

    pieces = (
        (k_in.at[0, 0, 0], 0, tokens),
        (v_in.at[0, 0, 0], tokens, tokens),
        (pk_in, low, pool_rows),
        (pv_in, low + pool_rows, pool_rows),
        (k_in.at[0, 0, 1], mid, tokens),
        (v_in.at[0, 0, 1], mid + tokens, tokens),
    )
    for source, start, size in pieces:
        pltpu.make_async_copy(source, mine.at[pl.ds(start, size)], load_sem).start()

    barrier = pltpu.get_barrier_semaphore()

    def greet(there, row, col):
        @pl.when(there)
        def _():
            pl.semaphore_signal(
                barrier, inc=1, device_id=(row, col), device_id_type=pl.DeviceIdType.MESH
            )

    pl.semaphore_signal(
        barrier, inc=1, device_id=(near_row, c), device_id_type=pl.DeviceIdType.MESH
    )
    greet(r + 2 < rows, r + 2, c)
    greet(r >= 2, r - 2, c)
    for step in range(1, cols):
        pl.semaphore_signal(
            barrier,
            inc=1,
            device_id=(r, lax.rem(c + step, cols)),
            device_id_type=pl.DeviceIdType.MESH,
        )

    ids_copy = pltpu.make_async_copy(ids_in, ids, ids_sem)
    ids_copy.start()
    tk_copy = pltpu.make_async_copy(tk_in.at[0], top_own.at[0], top_sem.at[0])
    tk_copy.start()
    tv_copy = pltpu.make_async_copy(tv_in.at[0], top_own.at[1], top_sem.at[1])
    tv_copy.start()
    q_copy = pltpu.make_async_copy(q_in.at[0, 0], q_buf, q_sem)
    q_copy.start()

    greeted = (
        1
        + (r + 2 < rows).astype(jnp.int32)
        + (r >= 2).astype(jnp.int32)
        + (cols - 1)
    )
    pl.semaphore_wait(barrier, greeted)

    def remote(source, target, send, recv, row, col):
        return pltpu.make_async_remote_copy(
            src_ref=source,
            dst_ref=target,
            send_sem=send,
            recv_sem=recv,
            device_id=(row, col),
            device_id_type=pl.DeviceIdType.MESH,
        )

    def near_copy(g):
        return remote(
            mine.at[:, lanes(g)], own.at[NEAR, g], near_send, near_recv.at[g], near_row, c
        )

    def far_copy(g):
        return remote(own.at[NEAR, g], own.at[FAR, g], far_send, far_recv.at[g], far_to, c)

    def to_left(k, g, n):
        return remote(
            own.at[k, pl.ds(g, n), pl.ds(0, edge)],
            right.at[k, pl.ds(g, n)],
            left_send.at[k],
            right_recv.at[k, g],
            r,
            c - 1,
        )

    def to_right(k, g, n):
        return remote(
            own.at[k, pl.ds(g, n), pl.ds(full - edge, edge)],
            left.at[k, pl.ds(g, n)],
            right_send.at[k],
            left_recv.at[k, g],
            r,
            c + 1,
        )

    def sideways(k, g, n):
        @pl.when(has_right)
        def _():
            to_right(k, g, n).start()

        @pl.when(has_left)
        def _():
            to_left(k, g, n).start()

    def piece(p):
        return pl.ds(pl.multiple_of(p * PAIR * width, PAIR * width), PAIR * width)

    def mine_to_left(p):
        return remote(
            mine.at[pl.ds(0, edge), piece(p)],
            mine_right.at[:, piece(p)],
            mine_send.at[0],
            mine_recv.at[1, p],
            r,
            c - 1,
        )

    def mine_to_right(p):
        return remote(
            mine.at[pl.ds(full - edge, edge), piece(p)],
            mine_left.at[:, piece(p)],
            mine_send.at[1],
            mine_recv.at[0, p],
            r,
            c + 1,
        )

    def mine_sideways(p):
        @pl.when(has_left)
        def _():
            mine_to_left(p).start()

        @pl.when(has_right)
        def _():
            mine_to_right(p).start()

    def top_copy(step):
        to = lax.rem(c + step, cols)
        return remote(top.at[c], top.at[c], top_send.at[step], top_recv.at[step], r, to)

    pltpu.make_async_copy(mine, mine, load_sem).wait()
    for g in range(min(AHEAD, chunks)):
        near_copy(g).start()

    mine_sideways(0)
    tk_copy.wait()
    tv_copy.wait()
    ids_copy.wait()
    top[c] = jnp.concatenate(
        [top_own[0].astype(jnp.float32), top_own[1].astype(jnp.float32)], axis=0
    ).astype(jnp.bfloat16)

    for step in range(1, cols):
        top_copy(step).start()

    @pl.when(jnp.logical_not(has_far))
    def _():
        own[FAR] = jnp.zeros(own.shape[1:], own.dtype)

    @pl.when(jnp.logical_not(has_far & has_left))
    def _():
        left[FAR] = jnp.zeros(left.shape[1:], left.dtype)

    @pl.when(jnp.logical_not(has_far & has_right))
    def _():
        right[FAR] = jnp.zeros(right.shape[1:], right.dtype)

    @pl.when(jnp.logical_not(has_left))
    def _():
        left[NEAR] = jnp.zeros(left.shape[1:], left.dtype)
        mine_left[...] = jnp.zeros(mine_left.shape, mine_left.dtype)

    @pl.when(jnp.logical_not(has_right))
    def _():
        right[NEAR] = jnp.zeros(right.shape[1:], right.dtype)
        mine_right[...] = jnp.zeros(mine_right.shape, mine_right.dtype)

    top_rows = cols * tk_in.shape[1]
    for b in range(2):
        beside = has_left if b == 0 else has_right
        far_beside = has_far & beside

        def fine(there, count):
            return jnp.full((1, count * tokens), jnp.where(there, 0.0, NEG_FILL), jnp.float32)

        shared = []
        for row, row_there, blocks in ((r, True, 1), (near_row, True, 2), (far_row, has_far, 2)):
            shared.append(fine(row_there, blocks))
            for shift in (-1, 0, 1):
                there = jnp.logical_and(row_there, (c + shift >= 0) & (c + shift < cols))
                base = (row * cols + c + shift) * pool_blocks
                for block in range(pool_blocks):
                    here = jnp.int32(0)
                    for n in range(ids.shape[3]):
                        here = here | (ids[0, 0, b, n] == base + block).astype(jnp.int32)
                    here = here * there.astype(jnp.int32)
                    value = (1.0 - here.astype(jnp.float32)) * NEG_FILL
                    shared.append(jnp.full((1, pool_tokens), value, jnp.float32))
        shared.append(jnp.zeros((1, top_rows), jnp.float32))
        private = [fine(beside, 2), fine(far_beside, 1), jnp.zeros((1, tokens), jnp.float32)]
        for target, parts in ((bias, shared), (side_bias, private)):
            at = 0
            for part in parts:
                target[b : b + 1, at : at + part.shape[1]] = part
                at += part.shape[1]

    q_copy.wait()

    score_scale = math.log2(math.e) / math.sqrt(head_width)

    def attend(g):
        at = lanes(g)
        q_chunk = q_buf[:, :, at].reshape(2 * tokens, width)
        tops = top[:, :, at].astype(jnp.float32)
        per = tk_in.shape[1]
        top_k = tops[:, :per].reshape(top_rows, width).astype(jnp.bfloat16)
        top_v = tops[:, per:].reshape(top_rows, width).astype(jnp.bfloat16)

        side = full - edge

        def pieces_of(head, value):
            lane = pl.ds(head * head_width, head_width)
            mine_lane = pl.ds(
                pl.multiple_of(g * width + head * head_width, head_width), head_width
            )
            fine = tokens if value else 0
            pool = pool_rows if value else 0
            top_part = top_v if value else top_k
            first = pl.ds(fine, tokens)
            second = pl.ds(mid + fine, tokens)
            left_block = pl.ds(mid + fine - side, tokens)
            left_pool = pl.ds(low + pool - side, pool_rows)
            pools = pl.ds(low + pool, pool_rows)
            mine_first = mine[first, mine_lane]
            shared = [
                mine[second, mine_lane],
                mine_left[left_pool, mine_lane],
                mine[pools, mine_lane],
                mine_right[pools, mine_lane],
            ]
            for k in (NEAR, FAR):
                shared += [
                    own[k, g, first, lane],
                    own[k, g, second, lane],
                    left[k, g, left_pool, lane],
                    own[k, g, pools, lane],
                    right[k, g, pools, lane],
                ]
            shared.append(top_part[:, head * head_width : (head + 1) * head_width])
            low_side = [
                mine_left[left_block, mine_lane],
                left[NEAR, g, left_block, lane],
                left[FAR, g, left_block, lane],
                mine_first,
            ]
            high_side = [
                mine_right[first, mine_lane],
                right[NEAR, g, first, lane],
                right[FAR, g, first, lane],
                mine_first,
            ]
            return [jnp.concatenate(part, axis=0) for part in (shared, low_side, high_side)]

        def product(x, y):
            return lax.dot_general(
                x, y, (((1,), (1,)), ((), ())), preferred_element_type=jnp.float32
            )

        def scores_of(head):
            q_head = q_chunk[:, head * head_width : (head + 1) * head_width]
            shared, low_side, high_side = pieces_of(head, False)
            both = product(q_head, shared).reshape(2, tokens, -1)
            alone = jnp.stack(
                [product(q_head[:tokens], low_side), product(q_head[tokens:], high_side)]
            )
            return (
                both * score_scale + bias[...][:, None, :],
                alone * score_scale + side_bias[...][:, None, :],
            )

        def weights_of(both, alone):
            peak = jnp.maximum(
                jnp.max(both, axis=-1, keepdims=True), jnp.max(alone, axis=-1, keepdims=True)
            )
            both = jnp.exp2(both - peak)
            alone = jnp.exp2(alone - peak)
            total = jnp.sum(both, axis=-1, keepdims=True) + jnp.sum(alone, axis=-1, keepdims=True)
            share = 1.0 / total
            return (both * share).astype(jnp.bfloat16), (alone * share).astype(jnp.bfloat16)

        def attended(head, both, alone):
            shared, low_side, high_side = pieces_of(head, True)
            result = jnp.dot(
                both.reshape(2 * tokens, -1), shared, preferred_element_type=jnp.float32
            ).reshape(2, tokens, head_width)
            result = result + jnp.stack(
                [
                    jnp.dot(alone[0], low_side, preferred_element_type=jnp.float32),
                    jnp.dot(alone[1], high_side, preferred_element_type=jnp.float32),
                ]
            )
            out_lane = pl.ds(
                pl.multiple_of(g * width + head * head_width, head_width), head_width
            )
            out[0, 0, :, :, out_lane] = result.astype(jnp.bfloat16)

        count = width // head_width
        scores = [scores_of(head) for head in range(count)]
        weights = [weights_of(*pair) for pair in scores]
        for head in range(count):
            attended(head, *weights[head])

    def step(t, _):
        @pl.when(t < chunks)
        def _():
            near_copy(t).wait_recv()

            @pl.when(has_to)
            def _():
                far_copy(t).start()

            @pl.when(lax.rem(t, PAIR) == PAIR - 1)
            def _():
                sideways(NEAR, t - (PAIR - 1), PAIR)

            @pl.when((lax.rem(t, PAIR) == PAIR - 1) & (t + 1 < chunks))
            def _():
                mine_sideways((t + 1) // PAIR)

        @pl.when(t + AHEAD < chunks)
        def _():
            near_copy(t + AHEAD).start()

        @pl.when(t >= ATTEND_LAG)
        def _():
            g = t - ATTEND_LAG

            @pl.when(g == 0)
            def _():
                for s in range(1, cols):
                    top_copy(s).wait_recv()

            first = lax.rem(g, PAIR) == 0

            @pl.when(first & has_left)
            def _():
                mine_to_right(g // PAIR).wait_recv()
                to_right(NEAR, g, PAIR).wait_recv()

            @pl.when(first & has_right)
            def _():
                mine_to_left(g // PAIR).wait_recv()
                to_left(NEAR, g, PAIR).wait_recv()

            @pl.when(has_far & has_left)
            def _():
                to_right(FAR, g, 1).wait_recv()

            @pl.when(has_far & has_right)
            def _():
                to_left(FAR, g, 1).wait_recv()

            attend(g)

        @pl.when((t >= FAR_LAG) & (t < chunks + FAR_LAG) & has_far)
        def _():
            far_copy(t - FAR_LAG).wait_recv()
            sideways(FAR, t - FAR_LAG, 1)

        return 0

    lax.fori_loop(0, chunks + ATTEND_LAG, step, 0)

    remote(own.at[NEAR], own.at[NEAR], near_send, near_recv.at[0], near_row, c).wait_send()

    @pl.when(has_to)
    def _():
        remote(own.at[NEAR], own.at[FAR], far_send, far_recv.at[0], far_to, c).wait_send()

    def sent(k):
        @pl.when(has_left)
        def _():
            remote(
                own.at[k, :, pl.ds(0, edge)],
                right.at[k],
                left_send.at[k],
                right_recv.at[k, 0],
                r,
                c - 1,
            ).wait_send()

        @pl.when(has_right)
        def _():
            remote(
                own.at[k, :, pl.ds(full - edge, edge)],
                left.at[k],
                right_send.at[k],
                left_recv.at[k, 0],
                r,
                c + 1,
            ).wait_send()

    @pl.when(has_left)
    def _():
        remote(
            mine_right, mine_right, mine_send.at[0], mine_recv.at[1, 0], r, c - 1
        ).wait_send()

    @pl.when(has_right)
    def _():
        remote(
            mine_left, mine_left, mine_send.at[1], mine_recv.at[0, 0], r, c + 1
        ).wait_send()

    sent(NEAR)

    @pl.when(has_far)
    def _():
        sent(FAR)

    for s in range(1, cols):
        top_copy(s).wait_send()


def solution(mesh):
    row_count, col_count = mesh.shape["row"], mesh.shape["col"]

    def body(queries, keys, values, pool_keys, pool_values, top_keys, top_values, coarse_ids):
        tokens, model_width = queries.shape[3:]
        pool_blocks, pool_tokens, _ = pool_keys.shape
        pool_rows = pool_blocks * pool_tokens
        head_width = model_width // HEADS
        width = HEADS_PER_CHUNK * head_width
        chunks = model_width // width
        full = 4 * tokens + 2 * pool_rows
        edge = 2 * tokens + 2 * pool_rows
        per = top_keys.shape[1]
        listed = 5 * tokens + 9 * pool_rows + col_count * per
        dims = (row_count, col_count, tokens, pool_rows, pool_blocks, chunks, width, head_width)
        dma = pltpu.SemaphoreType.DMA
        return pl.pallas_call(
            functools.partial(kernel, dims),
            out_shape=pltpu.VMEM(queries.shape, queries.dtype),
            in_specs=[pl.BlockSpec(memory_space=pltpu.HBM)] * 8,
            out_specs=pl.BlockSpec(memory_space=pltpu.VMEM),
            scratch_shapes=[
                pltpu.VMEM((full, model_width), jnp.bfloat16),
                pltpu.VMEM((edge, model_width), jnp.bfloat16),
                pltpu.VMEM((edge, model_width), jnp.bfloat16),
                pltpu.VMEM((2, chunks, full, width), jnp.bfloat16),
                pltpu.VMEM((2, chunks, edge, width), jnp.bfloat16),
                pltpu.VMEM((2, chunks, edge, width), jnp.bfloat16),
                pltpu.VMEM((2, tokens, model_width), jnp.bfloat16),
                pltpu.VMEM((col_count, 2 * per, model_width), jnp.bfloat16),
                pltpu.VMEM((2, per, model_width), jnp.bfloat16),
                pltpu.SMEM(coarse_ids.shape, jnp.int32),
                pltpu.VMEM((2, listed), jnp.float32),
                pltpu.VMEM((2, 4 * tokens), jnp.float32),
                dma,
                dma((2,)),
                dma,
                dma,
                dma,
                dma((chunks,)),
                dma,
                dma((chunks,)),
                dma((2,)),
                dma((2, chunks)),
                dma((2,)),
                dma((2, chunks)),
                dma((2,)),
                dma((2, chunks // PAIR)),
                dma((col_count,)),
                dma((col_count,)),
            ],
            compiler_params=pltpu.CompilerParams(
                collective_id=0, has_side_effects=True, vmem_limit_bytes=62 * 2**20
            ),
            cost_estimate=pl.CostEstimate(
                flops=4 * 2 * tokens * (listed + 4 * tokens) * model_width,
                bytes_accessed=8 * 2**20,
                transcendentals=2 * tokens * (listed + 4 * tokens) * HEADS,
            ),
        )(
            queries,
            keys,
            values,
            pool_keys.reshape(pool_rows, model_width),
            pool_values.reshape(pool_rows, model_width),
            top_keys,
            top_values,
            coarse_ids,
        )

    placed = (
        P(None, "row", "col", None, None),
        P(None, "row", "col", None, None),
        P(None, "row", "col", None, None),
        P(("row", "col"), None, None),
        P(("row", "col"), None, None),
        P(None, "col", None),
        P(None, "col", None),
        P(None, "row", "col", None),
    )
    return jax.shard_map(
        body,
        mesh=mesh,
        in_specs=placed,
        out_specs=P(None, "row", "col", None, None),
        check_vma=False,
    )
```

```python
import functools
import math

import jax
import jax.numpy as jnp
from jax import lax
from jax.experimental import pallas as pl
from jax.experimental.pallas import tpu as pltpu
from jax.sharding import PartitionSpec as P

HEADS = 16
NEG_FILL = -1e30
HEADS_PER_CHUNK = 2
AHEAD = 3
FAR_LAG = 1
ATTEND_LAG = 3
PAIR = 2
NEAR, FAR = 0, 1


def kernel(
    dims,
    q_in,
    k_in,
    v_in,
    pk_in,
    pv_in,
    tk_in,
    tv_in,
    ids_in,
    out,
    mine,
    pack,
    mine_left,
    mine_right,
    own,
    left,
    right,
    q_buf,
    top,
    top_own,
    ids,
    bias,
    side_bias,
    load_sem,
    pack_sem,
    top_sem,
    ids_sem,
    q_sem,
    near_send,
    near_recv,
    far_send,
    far_recv,
    left_send,
    left_recv,
    right_send,
    right_recv,
    mine_send,
    mine_recv,
    top_send,
    top_recv,
):
    rows, cols, tokens, pool_rows, pool_blocks, chunks, width, head_width = dims
    pool_tokens = pool_rows // pool_blocks
    r = lax.axis_index("row")
    c = lax.axis_index("col")
    odd = lax.rem(r, 2)
    near_row = r + 1 - 2 * odd
    far_row = r - 1 + 2 * odd
    far_to = r + 2 - 4 * odd
    has_far = (far_row >= 0) & (far_row < rows)
    has_to = (far_to >= 0) & (far_to < rows)
    has_left = c > 0
    has_right = c < cols - 1
    low = 2 * tokens
    mid = low + 2 * pool_rows
    full = mid + 2 * tokens
    edge = mid

    def lanes(g):
        return pl.ds(pl.multiple_of(g * width, width), width)

    pieces = (
        (k_in.at[0, 0, 0], 0, tokens),
        (v_in.at[0, 0, 0], tokens, tokens),
        (pk_in, low, pool_rows),
        (pv_in, low + pool_rows, pool_rows),
        (k_in.at[0, 0, 1], mid, tokens),
        (v_in.at[0, 0, 1], mid + tokens, tokens),
    )
    for source, start, size in pieces:
        pltpu.make_async_copy(source, mine.at[pl.ds(start, size)], load_sem).start()

    barrier = pltpu.get_barrier_semaphore()

    def greet(there, row, col):
        @pl.when(there)
        def _():
            pl.semaphore_signal(
                barrier, inc=1, device_id=(row, col), device_id_type=pl.DeviceIdType.MESH
            )

    pl.semaphore_signal(
        barrier, inc=1, device_id=(near_row, c), device_id_type=pl.DeviceIdType.MESH
    )
    greet(r + 2 < rows, r + 2, c)
    greet(r >= 2, r - 2, c)
    for step in range(1, cols):
        pl.semaphore_signal(
            barrier,
            inc=1,
            device_id=(r, lax.rem(c + step, cols)),
            device_id_type=pl.DeviceIdType.MESH,
        )

    ids_copy = pltpu.make_async_copy(ids_in, ids, ids_sem)
    ids_copy.start()
    tk_copy = pltpu.make_async_copy(tk_in.at[0], top_own.at[0], top_sem.at[0])
    tk_copy.start()
    tv_copy = pltpu.make_async_copy(tv_in.at[0], top_own.at[1], top_sem.at[1])
    tv_copy.start()
    q_copy = pltpu.make_async_copy(q_in.at[0, 0], q_buf, q_sem)
    q_copy.start()

    greeted = (
        1
        + (r + 2 < rows).astype(jnp.int32)
        + (r >= 2).astype(jnp.int32)
        + (cols - 1)
    )
    pl.semaphore_wait(barrier, greeted)

    def remote(source, target, send, recv, row, col):
        return pltpu.make_async_remote_copy(
            src_ref=source,
            dst_ref=target,
            send_sem=send,
            recv_sem=recv,
            device_id=(row, col),
            device_id_type=pl.DeviceIdType.MESH,
        )

    def near_copy(g):
        return remote(
            pack.at[g], own.at[NEAR, g], near_send, near_recv.at[g], near_row, c
        )

    def far_copy(g):
        return remote(own.at[NEAR, g], own.at[FAR, g], far_send, far_recv.at[g], far_to, c)

    def to_left(k, g, n):
        return remote(
            own.at[k, pl.ds(g, n), pl.ds(0, edge)],
            right.at[k, pl.ds(g, n)],
            left_send.at[k],
            right_recv.at[k, g],
            r,
            c - 1,
        )

    def to_right(k, g, n):
        return remote(
            own.at[k, pl.ds(g, n), pl.ds(full - edge, edge)],
            left.at[k, pl.ds(g, n)],
            right_send.at[k],
            left_recv.at[k, g],
            r,
            c + 1,
        )

    def sideways(k, g, n):
        @pl.when(has_left)
        def _():
            to_left(k, g, n).start()

        @pl.when(has_right)
        def _():
            to_right(k, g, n).start()

    mine_to_left = remote(
        mine.at[pl.ds(0, edge)], mine_right, mine_send.at[0], mine_recv.at[1], r, c - 1
    )
    mine_to_right = remote(
        mine.at[pl.ds(full - edge, edge)], mine_left, mine_send.at[1], mine_recv.at[0], r, c + 1
    )

    def top_copy(step):
        to = lax.rem(c + step, cols)
        return remote(top.at[c], top.at[c], top_send.at[step], top_recv.at[step], r, to)

    pltpu.make_async_copy(mine, mine, load_sem).wait()

    def pack_copy(g):
        return pltpu.make_async_copy(mine.at[:, lanes(g)], pack.at[g], pack_sem.at[g])

    def send_near(g):
        pack_copy(g).wait()
        near_copy(g).start()

    for g in range(chunks):
        pack_copy(g).start()
    for g in range(min(AHEAD, chunks)):
        send_near(g)

    @pl.when(has_left)
    def _():
        mine_to_left.start()

    @pl.when(has_right)
    def _():
        mine_to_right.start()

    tk_copy.wait()
    tv_copy.wait()
    ids_copy.wait()
    top[c] = jnp.concatenate(
        [top_own[0].astype(jnp.float32), top_own[1].astype(jnp.float32)], axis=0
    ).astype(jnp.bfloat16)

    for step in range(1, cols):
        top_copy(step).start()

    @pl.when(jnp.logical_not(has_far))
    def _():
        own[FAR] = jnp.zeros(own.shape[1:], own.dtype)

    @pl.when(jnp.logical_not(has_far & has_left))
    def _():
        left[FAR] = jnp.zeros(left.shape[1:], left.dtype)

    @pl.when(jnp.logical_not(has_far & has_right))
    def _():
        right[FAR] = jnp.zeros(right.shape[1:], right.dtype)

    @pl.when(jnp.logical_not(has_left))
    def _():
        left[NEAR] = jnp.zeros(left.shape[1:], left.dtype)
        mine_left[...] = jnp.zeros(mine_left.shape, mine_left.dtype)

    @pl.when(jnp.logical_not(has_right))
    def _():
        right[NEAR] = jnp.zeros(right.shape[1:], right.dtype)
        mine_right[...] = jnp.zeros(mine_right.shape, mine_right.dtype)

    top_rows = cols * tk_in.shape[1]
    for b in range(2):
        beside = has_left if b == 0 else has_right
        far_beside = has_far & beside

        def fine(there, count):
            return jnp.full((1, count * tokens), jnp.where(there, 0.0, NEG_FILL), jnp.float32)

        shared = []
        for row, row_there, blocks in ((r, True, 1), (near_row, True, 2), (far_row, has_far, 2)):
            shared.append(fine(row_there, blocks))
            for shift in (-1, 0, 1):
                there = jnp.logical_and(row_there, (c + shift >= 0) & (c + shift < cols))
                base = (row * cols + c + shift) * pool_blocks
                for block in range(pool_blocks):
                    here = jnp.int32(0)
                    for n in range(ids.shape[3]):
                        here = here | (ids[0, 0, b, n] == base + block).astype(jnp.int32)
                    here = here * there.astype(jnp.int32)
                    value = (1.0 - here.astype(jnp.float32)) * NEG_FILL
                    shared.append(jnp.full((1, pool_tokens), value, jnp.float32))
        shared.append(jnp.zeros((1, top_rows), jnp.float32))
        private = [fine(beside, 2), fine(far_beside, 1), jnp.zeros((1, tokens), jnp.float32)]
        for target, parts in ((bias, shared), (side_bias, private)):
            at = 0
            for part in parts:
                target[b : b + 1, at : at + part.shape[1]] = part
                at += part.shape[1]

    q_copy.wait()

    score_scale = math.log2(math.e) / math.sqrt(head_width)

    def attend(g):
        at = lanes(g)
        q_chunk = q_buf[:, :, at].reshape(2 * tokens, width)
        tops = top[:, :, at].astype(jnp.float32)
        per = tk_in.shape[1]
        top_k = tops[:, :per].reshape(top_rows, width).astype(jnp.bfloat16)
        top_v = tops[:, per:].reshape(top_rows, width).astype(jnp.bfloat16)

        side = full - edge

        def pieces_of(head, value):
            lane = pl.ds(head * head_width, head_width)
            mine_lane = pl.ds(
                pl.multiple_of(g * width + head * head_width, head_width), head_width
            )
            fine = tokens if value else 0
            pool = pool_rows if value else 0
            top_part = top_v if value else top_k
            first = pl.ds(fine, tokens)
            second = pl.ds(mid + fine, tokens)
            left_block = pl.ds(mid + fine - side, tokens)
            left_pool = pl.ds(low + pool - side, pool_rows)
            pools = pl.ds(low + pool, pool_rows)
            mine_first = mine[first, mine_lane]
            shared = [
                mine[second, mine_lane],
                mine_left[left_pool, mine_lane],
                mine[pools, mine_lane],
                mine_right[pools, mine_lane],
            ]
            for k in (NEAR, FAR):
                shared += [
                    own[k, g, first, lane],
                    own[k, g, second, lane],
                    left[k, g, left_pool, lane],
                    own[k, g, pools, lane],
                    right[k, g, pools, lane],
                ]
            shared.append(top_part[:, head * head_width : (head + 1) * head_width])
            low_side = [
                mine_left[left_block, mine_lane],
                left[NEAR, g, left_block, lane],
                left[FAR, g, left_block, lane],
                mine_first,
            ]
            high_side = [
                mine_right[first, mine_lane],
                right[NEAR, g, first, lane],
                right[FAR, g, first, lane],
                mine_first,
            ]
            return [jnp.concatenate(part, axis=0) for part in (shared, low_side, high_side)]

        def product(x, y):
            return lax.dot_general(
                x, y, (((1,), (1,)), ((), ())), preferred_element_type=jnp.float32
            )

        def scores_of(head):
            q_head = q_chunk[:, head * head_width : (head + 1) * head_width]
            shared, low_side, high_side = pieces_of(head, False)
            both = product(q_head, shared).reshape(2, tokens, -1)
            alone = jnp.stack(
                [product(q_head[:tokens], low_side), product(q_head[tokens:], high_side)]
            )
            return (
                both * score_scale + bias[...][:, None, :],
                alone * score_scale + side_bias[...][:, None, :],
            )

        def weights_of(both, alone):
            peak = jnp.maximum(
                jnp.max(both, axis=-1, keepdims=True), jnp.max(alone, axis=-1, keepdims=True)
            )
            both = jnp.exp2(both - peak)
            alone = jnp.exp2(alone - peak)
            total = jnp.sum(both, axis=-1, keepdims=True) + jnp.sum(alone, axis=-1, keepdims=True)
            share = 1.0 / total
            return (both * share).astype(jnp.bfloat16), (alone * share).astype(jnp.bfloat16)

        def attended(head, both, alone):
            shared, low_side, high_side = pieces_of(head, True)
            result = jnp.dot(
                both.reshape(2 * tokens, -1), shared, preferred_element_type=jnp.float32
            ).reshape(2, tokens, head_width)
            result = result + jnp.stack(
                [
                    jnp.dot(alone[0], low_side, preferred_element_type=jnp.float32),
                    jnp.dot(alone[1], high_side, preferred_element_type=jnp.float32),
                ]
            )
            out_lane = pl.ds(
                pl.multiple_of(g * width + head * head_width, head_width), head_width
            )
            out[0, 0, :, :, out_lane] = result.astype(jnp.bfloat16)

        count = width // head_width
        scores = [scores_of(head) for head in range(count)]
        weights = [weights_of(*pair) for pair in scores]
        for head in range(count):
            attended(head, *weights[head])

    def step(t, _):
        @pl.when(t < chunks)
        def _():
            near_copy(t).wait_recv()

            @pl.when(has_to)
            def _():
                far_copy(t).start()

            @pl.when(lax.rem(t, PAIR) == PAIR - 1)
            def _():
                sideways(NEAR, t - (PAIR - 1), PAIR)

        @pl.when(t + AHEAD < chunks)
        def _():
            send_near(t + AHEAD)

        @pl.when(t >= ATTEND_LAG)
        def _():
            g = t - ATTEND_LAG

            @pl.when(g == 0)
            def _():
                for s in range(1, cols):
                    top_copy(s).wait_recv()

            @pl.when((g == 0) & has_left)
            def _():
                mine_to_right.wait_recv()

            @pl.when((g == 0) & has_right)
            def _():
                mine_to_left.wait_recv()

            first = lax.rem(g, PAIR) == 0

            @pl.when(first & has_left)
            def _():
                to_right(NEAR, g, PAIR).wait_recv()

            @pl.when(first & has_right)
            def _():
                to_left(NEAR, g, PAIR).wait_recv()

            @pl.when(has_far & has_left)
            def _():
                to_right(FAR, g, 1).wait_recv()

            @pl.when(has_far & has_right)
            def _():
                to_left(FAR, g, 1).wait_recv()

            attend(g)

        @pl.when((t >= FAR_LAG) & (t < chunks + FAR_LAG) & has_far)
        def _():
            far_copy(t - FAR_LAG).wait_recv()
            sideways(FAR, t - FAR_LAG, 1)

        return 0

    lax.fori_loop(0, chunks + ATTEND_LAG, step, 0)

    remote(own.at[NEAR], own.at[NEAR], near_send, near_recv.at[0], near_row, c).wait_send()

    @pl.when(has_to)
    def _():
        remote(own.at[NEAR], own.at[FAR], far_send, far_recv.at[0], far_to, c).wait_send()

    def sent(k):
        @pl.when(has_left)
        def _():
            remote(
                own.at[k, :, pl.ds(0, edge)],
                right.at[k],
                left_send.at[k],
                right_recv.at[k, 0],
                r,
                c - 1,
            ).wait_send()

        @pl.when(has_right)
        def _():
            remote(
                own.at[k, :, pl.ds(full - edge, edge)],
                left.at[k],
                right_send.at[k],
                left_recv.at[k, 0],
                r,
                c + 1,
            ).wait_send()

    @pl.when(has_left)
    def _():
        mine_to_left.wait_send()

    @pl.when(has_right)
    def _():
        mine_to_right.wait_send()

    sent(NEAR)

    @pl.when(has_far)
    def _():
        sent(FAR)

    for s in range(1, cols):
        top_copy(s).wait_send()


def solution(mesh):
    row_count, col_count = mesh.shape["row"], mesh.shape["col"]

    def body(queries, keys, values, pool_keys, pool_values, top_keys, top_values, coarse_ids):
        tokens, model_width = queries.shape[3:]
        pool_blocks, pool_tokens, _ = pool_keys.shape
        pool_rows = pool_blocks * pool_tokens
        head_width = model_width // HEADS
        width = HEADS_PER_CHUNK * head_width
        chunks = model_width // width
        full = 4 * tokens + 2 * pool_rows
        edge = 2 * tokens + 2 * pool_rows
        per = top_keys.shape[1]
        listed = 5 * tokens + 9 * pool_rows + col_count * per
        dims = (row_count, col_count, tokens, pool_rows, pool_blocks, chunks, width, head_width)
        dma = pltpu.SemaphoreType.DMA
        return pl.pallas_call(
            functools.partial(kernel, dims),
            out_shape=pltpu.VMEM(queries.shape, queries.dtype),
            in_specs=[pl.BlockSpec(memory_space=pltpu.HBM)] * 8,
            out_specs=pl.BlockSpec(memory_space=pltpu.VMEM),
            scratch_shapes=[
                pltpu.VMEM((full, model_width), jnp.bfloat16),
                pltpu.VMEM((chunks, full, width), jnp.bfloat16),
                pltpu.VMEM((edge, model_width), jnp.bfloat16),
                pltpu.VMEM((edge, model_width), jnp.bfloat16),
                pltpu.VMEM((2, chunks, full, width), jnp.bfloat16),
                pltpu.VMEM((2, chunks, edge, width), jnp.bfloat16),
                pltpu.VMEM((2, chunks, edge, width), jnp.bfloat16),
                pltpu.VMEM((2, tokens, model_width), jnp.bfloat16),
                pltpu.VMEM((col_count, 2 * per, model_width), jnp.bfloat16),
                pltpu.VMEM((2, per, model_width), jnp.bfloat16),
                pltpu.SMEM(coarse_ids.shape, jnp.int32),
                pltpu.VMEM((2, listed), jnp.float32),
                pltpu.VMEM((2, 4 * tokens), jnp.float32),
                dma,
                dma((chunks,)),
                dma((2,)),
                dma,
                dma,
                dma,
                dma((chunks,)),
                dma,
                dma((chunks,)),
                dma((2,)),
                dma((2, chunks)),
                dma((2,)),
                dma((2, chunks)),
                dma((2,)),
                dma((2,)),
                dma((col_count,)),
                dma((col_count,)),
            ],
            compiler_params=pltpu.CompilerParams(
                collective_id=0, has_side_effects=True, vmem_limit_bytes=62 * 2**20
            ),
            cost_estimate=pl.CostEstimate(
                flops=4 * 2 * tokens * (listed + 4 * tokens) * model_width,
                bytes_accessed=8 * 2**20,
                transcendentals=2 * tokens * (listed + 4 * tokens) * HEADS,
            ),
        )(
            queries,
            keys,
            values,
            pool_keys.reshape(pool_rows, model_width),
            pool_values.reshape(pool_rows, model_width),
            top_keys,
            top_values,
            coarse_ids,
        )

    placed = (
        P(None, "row", "col", None, None),
        P(None, "row", "col", None, None),
        P(None, "row", "col", None, None),
        P(("row", "col"), None, None),
        P(("row", "col"), None, None),
        P(None, "col", None),
        P(None, "col", None),
        P(None, "row", "col", None),
    )
    return jax.shard_map(
        body,
        mesh=mesh,
        in_specs=placed,
        out_specs=P(None, "row", "col", None, None),
        check_vma=False,
    )
```
